256 devices in a mesh: ctx: 32 (over x, z), head: 8 (over y, core).
Axes of the slice: x: 4, y: 4, z: 8, core: 2. Of those that a mesh axis runs over, the one named last changes fastest.
Arguments:
- query: bfloat16 [32768, 8192], P('ctx', 'head'), may hold values from -6 to 6
- key_in: bfloat16 [32768, 8192], P('ctx', 'head'), may hold values from -6 to 6
- value_in: bfloat16 [32768, 8192], P('ctx', 'head'), may hold values from -6 to 6
- gate_in: bfloat16 [32768, 8192], P('ctx', 'head'), may hold values from -6 to 6
- norm_gain: float32 [8192], P('head'), may hold values from 0.1 to 1.9
- decay_rate: float32 [64], P('head'), may hold values from 0 to 1, as said below
- request_starts: int32 [32], replicated, may hold values from 0 to 32767, as said below
- request_slots: int32 [32], replicated, may hold values from 0 to 31, each once
Outputs:
- normed_output: bfloat16 [32768, 8192], P('ctx', 'head')
- final_states: bfloat16 [32, 64, 128, 128], P('ctx', 'head')
The draws below stay inside these ranges and needn't reach their ends.
Inputs may be any that keep to these rules, and one draw needn't show every extreme that they name: request_starts rises, its first entry is 0, and the last request runs to the stream's last token. Each aligned block of 1024 tokens holds the last tokens of at most 2 requests, and some block holds exactly 2. `request_slots`: each value once. Request r's decode owner is ctx rank request_slots[r]. `decay_rate`: positive rates.
All inputs are finite; a program needn't handle non-finite values.
Results may differ from the reference program's by a relative error of at most 0.0034.
Values may be sent and summed in bfloat16 or wider, within the bound.
No kernel may reach another device: no remote copies, remote signals or barrier semaphores. Data moves between devices by JAX's collectives and lax.ppermute only.
A program may use at most 128 MiB of HBM per device.

```python
import jax
import jax.numpy as jnp
from jax import lax

H = 64
E = 128
TOK_DEV = 1024
ENDS_MOST = 2
BLOCK = 512
TOKENS = 32768
NREQ = 32


def draw_decay_rate(key, part):
    key = jax.random.fold_in(key, 7)
    kind_key, level_key = jax.random.split(key, 2)
    slow_share = 0.5
    slow_low = 0.2 / TOKENS
    slow_high = 2.0 / TOKENS
    is_slow = jax.random.uniform(kind_key, (H,), jnp.float32) < slow_share
    level = jax.random.uniform(level_key, (H,), jnp.float32)
    slow_rate = jnp.exp(jnp.log(slow_low) + level * (jnp.log(slow_high) - jnp.log(slow_low)))
    fast_rate = jnp.exp(jnp.log(1.0 / 40.0) + level * (jnp.log(1.0 / 8.0) - jnp.log(1.0 / 40.0)))
    return jnp.where(is_slow, slow_rate, fast_rate).astype(jnp.float32)


def draw_request_starts(key, part):
    key = jax.random.fold_in(key, 11)
    split_key, order_key, quiet_key, place_key = jax.random.split(key, 4)
    device_total = TOKENS // TOK_DEV
    quiet_total = device_total // 4
    pair_total = (device_total - 2 * quiet_total) // 2
    first_counts = jax.random.randint(split_key, (pair_total,), 0, ENDS_MOST + 1).astype(jnp.int32)
    paired = jnp.concatenate([first_counts, ENDS_MOST - first_counts])
    donors = jnp.full((quiet_total - 1,), ENDS_MOST, jnp.int32)
    movable = jax.random.permutation(order_key, jnp.concatenate([donors, paired]))
    placed = jnp.concatenate([movable, jnp.full((1,), ENDS_MOST, jnp.int32)])
    quiet_start = jax.random.randint(quiet_key, (), 0, device_total - quiet_total)
    rank_ids = jnp.arange(device_total)
    source = jnp.where(rank_ids < quiet_start, rank_ids, rank_ids - quiet_total)
    source = jnp.clip(source, 0, device_total - quiet_total - 1)
    inside = (rank_ids >= quiet_start) & (rank_ids < quiet_start + quiet_total)
    device_counts = jnp.where(inside, 0, placed[source]).astype(jnp.int32)
    device_keys = jax.random.split(place_key, device_total)
    shuffled = jax.vmap(lambda one_key: jax.random.permutation(one_key, TOK_DEV)[:ENDS_MOST])(device_keys)
    slot_ids = jnp.arange(ENDS_MOST)
    valid = slot_ids[None, :] < device_counts[:, None]
    marked = jnp.where(valid, shuffled, TOK_DEV)
    ordered = jnp.sort(marked, axis=1)
    last_count = device_counts[device_total - 1]
    ordered = ordered.at[device_total - 1, last_count - 1].set(TOK_DEV - 1)
    device_base = jnp.arange(device_total)[:, None] * TOK_DEV
    global_ends = jnp.where(ordered < TOK_DEV, ordered + device_base, TOKENS)
    flat_ends = jnp.sort(global_ends.reshape(-1))[:NREQ]
    return jnp.concatenate([jnp.zeros((1,), jnp.int32), (flat_ends[:-1] + 1).astype(jnp.int32)]).astype(jnp.int32)


def block_levels(rng, shape, cuts, least, top_value):
    loudness, own = 1.0, jax.random.fold_in(rng, 6)
    for dim, parts in cuts:
        draws = jnp.exp(jax.random.uniform(jax.random.fold_in(own, dim), (parts,), jnp.float32, least / len(cuts), top_value / len(cuts)))
        loudness = loudness * jnp.repeat(draws, shape[dim] // parts).reshape([-1 if axis == dim else 1 for axis in range(len(shape))])
    return loudness


def gaussian(own_key, extent, spread, bound, shards=(), held_as=jnp.bfloat16):
    factor_of = block_levels(own_key, extent, shards, -0.22, 0.18) if shards else 1.0
    array = jax.random.normal(own_key, extent, jnp.float32) * spread * factor_of
    return jnp.minimum(jnp.maximum(array, -bound), bound).astype(held_as)


def setup_inputs(seed: int = 0) -> dict:
    splits = jax.random.split(jax.random.key(seed), 9)
    return {
        "query": gaussian(splits[0], (TOKENS, H * E), 1.0, 6.0, ((0, 32), (1, 8))),
        "key_in": gaussian(splits[1], (TOKENS, H * E), 1.0, 6.0, ((0, 32), (1, 8))),
        "value_in": gaussian(splits[2], (TOKENS, H * E), 1.0, 6.0, ((0, 32), (1, 8))),
        "gate_in": gaussian(splits[3], (TOKENS, H * E), 1.0, 6.0, ((0, 32), (1, 8))),
        "norm_gain": jnp.clip(1.0 + 0.18 * jax.random.normal(splits[4], (H * E,), jnp.float32), 0.1, 1.9),
        "decay_rate": draw_decay_rate(jax.random.fold_in(splits[8], 71), 0),
        "request_starts": draw_request_starts(jax.random.fold_in(splits[8], 71), 0),
        "request_slots": jax.random.permutation(splits[7], NREQ).astype(jnp.int32),
    }


norm_eps = 1e-06

def activate(values):
    widened = values.astype(jnp.float32)
    return (widened * jax.nn.sigmoid(widened)).astype(jnp.bfloat16)

def narrow(values):
    return lax.optimization_barrier(values.astype(jnp.bfloat16)).astype(jnp.float32)

def reference(query, key_in, value_in, gate_in, norm_gain, decay_rate, request_starts, request_slots):
    highest = lax.Precision.HIGHEST
    stream = query.shape[0]
    blocks = stream // BLOCK
    queries = activate(query).reshape(blocks, BLOCK, H, E)
    keys_act = activate(key_in).reshape(blocks, BLOCK, H, E)
    values_act = activate(value_in).reshape(blocks, BLOCK, H, E)
    gates = gate_in.reshape(blocks, BLOCK, H * E)
    starts = request_starts.astype(jnp.int32)
    req_ends = jnp.concatenate([starts[1:] - 1, jnp.full((1,), stream - 1, jnp.int32)]).astype(jnp.int32)
    positions = jnp.arange(stream, dtype=jnp.int32)
    segment = (lax.optimization_barrier(jnp.sum((starts[None, :] <= positions[:, None]).astype(jnp.int32), axis=1)) - 1).astype(jnp.int32)
    seg_blocks = segment.reshape(blocks, BLOCK)
    rates = decay_rate.astype(jnp.float32)
    offsets = jnp.arange(BLOCK, dtype=jnp.int32)
    distance = offsets[:, None] - offsets[None, :]
    causal = distance >= 0
    decay_table = jnp.exp(-rates[:, None, None] * jnp.maximum(distance, 0).astype(jnp.float32)[None])
    gain = norm_gain.astype(jnp.float32)

    def advance(carry, block):
        kv_state, finals = carry
        block_index, block_q, block_k, block_v, block_seg, block_gate = block
        first_token = (block_index * BLOCK).astype(jnp.int32)
        before = jnp.where(block_index > 0, segment[jnp.maximum(first_token - 1, 0)], -1).astype(jnp.int32)
        q_wide = block_q.astype(jnp.float32)
        k_wide = block_k.astype(jnp.float32)
        v_wide = block_v.astype(jnp.float32)
        same_req = ((block_seg[:, None] == block_seg[None, :]) & causal).astype(jnp.float32)
        scores = jnp.einsum('thd,shd->hts', q_wide, k_wide, precision=highest)
        weights = narrow(scores * decay_table * same_req[None])
        inner = jnp.einsum('hts,she->the', weights, v_wide, precision=highest)
        carried = (block_seg == before).astype(jnp.float32)
        reach = jnp.exp(-rates[None, :] * (offsets[:, None] + 1).astype(jnp.float32)) * carried[:, None]
        outer = jnp.einsum('thd,hde->the', q_wide, narrow(kv_state), precision=highest) * reach[:, :, None]
        attended = inner + outer
        mean_sq = lax.optimization_barrier(jnp.mean(attended * attended, axis=(1, 2)))
        scaled = (attended * lax.rsqrt(mean_sq + norm_eps)[:, None, None]).reshape(BLOCK, H * E)
        output = (scaled * gain[None, :] * jax.nn.sigmoid(block_gate.astype(jnp.float32))).astype(jnp.bfloat16)
        last_seg = block_seg[BLOCK - 1]
        keep = jnp.exp(-rates * float(BLOCK)) * (last_seg == before).astype(jnp.float32)
        tail = (BLOCK - 1 - offsets).astype(jnp.float32)
        key_weight = jnp.exp(-rates[None, :] * tail[:, None]) * (block_seg == last_seg).astype(jnp.float32)[:, None]
        update = jnp.einsum('shd,she->hde', narrow(k_wide * key_weight[:, :, None]), v_wide, precision=highest)
        earlier = jnp.sum((req_ends < first_token).astype(jnp.int32)).astype(jnp.int32)
        for end_index in range(ENDS_MOST):
            request = earlier + end_index
            safe = jnp.minimum(request, NREQ - 1).astype(jnp.int32)
            end_pos = req_ends[safe]
            valid = ((request < NREQ) & (end_pos < first_token + BLOCK)).astype(jnp.float32)
            gap = (end_pos - first_token - offsets).astype(jnp.int32)
            chosen = ((gap >= 0) & (block_seg == safe)).astype(jnp.float32)
            end_weight = jnp.exp(-rates[None, :] * jnp.maximum(gap, 0).astype(jnp.float32)[:, None]) * chosen[:, None]
            part = jnp.einsum('shd,she->hde', narrow(k_wide * end_weight[:, :, None]), v_wide, precision=highest)
            lead = jnp.exp(-rates * (end_pos - first_token + 1).astype(jnp.float32)) * (safe == before).astype(jnp.float32)
            whole = (lead[:, None, None] * kv_state + part) * valid
            finals = finals.at[request_slots[safe]].add(whole)
        new_state = keep[:, None, None] * kv_state + update
        return ((new_state, finals), output)
    initial = (jnp.zeros((H, E, E), jnp.float32), jnp.zeros((NREQ, H, E, E), jnp.float32))
    block_ids = jnp.arange(blocks, dtype=jnp.int32)
    (last_state, finals), outputs = lax.scan(advance, initial, (block_ids, queries, keys_act, values_act, seg_blocks, gates))
    return (outputs.reshape(stream, H * E), finals.astype(jnp.bfloat16))
```

```python
import functools

import jax
import jax.numpy as jnp
from jax import lax
from jax.experimental import pallas as pl
from jax.experimental.pallas import tpu as pltpu
from jax.sharding import PartitionSpec as P

E = 128
ENDS_MOST = 2
SEGS = ENDS_MOST + 1
BLOCK = 512
TILE = 256
ABSENT = 1 << 20
FAR = 1e38
norm_eps = 1e-06
MIB = 1 << 20
f32 = jnp.float32
bf16 = jnp.bfloat16
SMEM = pl.BlockSpec(memory_space=pltpu.SMEM)


def silu(values):
    half = values.astype(f32) * 0.5
    return (half + half * jnp.tanh(half)).astype(bf16)


def rate_of(rates_ref, head):
    return jnp.maximum(rates_ref[head], 1e-30)


def end_of(starts_ref, request, stream):
    count = starts_ref.shape[0]
    following = starts_ref[jnp.minimum(request + 1, count - 1)]
    return jnp.where(request < count - 1, following - 1, stream - 1)


def local_ends(starts_ref, rows, ranks):
    stream = rows * ranks
    offset = lax.axis_index("ctx") * rows
    count = starts_ref.shape[0]
    first = jnp.int32(0)
    for request in range(count - 1):
        first += (starts_ref[request + 1] - 1 < offset).astype(jnp.int32)
    end_a = end_of(starts_ref, first, stream) - offset
    end_b = end_of(starts_ref, first + 1, stream) - offset
    end_b = jnp.where(first + 1 < count, end_b, ABSENT)
    return end_a, end_b


def scalar_exp(value):
    return jnp.exp(jnp.full((1, E), value, f32))


def states_kernel(rows, ranks, starts_ref, rates_ref, k_ref, v_ref, sums_ref, mid_ref, gap, masks):
    head = pl.program_id(0)
    end_a, end_b = local_ends(starts_ref, rows, ranks)

    @pl.when(head == 0)
    def _():
        token = lax.broadcasted_iota(jnp.int32, (rows, E), 0)
        seg_end = jnp.where(token <= end_a, end_a, jnp.where(token <= end_b, end_b, ABSENT))
        block_end = (token // BLOCK) * BLOCK + (BLOCK - 1)
        gap[...] = (jnp.minimum(seg_end, block_end) - token).astype(f32)
        in_a = token <= end_a
        in_b = token <= end_b
        masks[0] = jnp.where(in_a, 1.0, 0.0).astype(bf16)
        masks[1] = jnp.where(in_b, jnp.where(in_a, 0.0, 1.0), 0.0).astype(bf16)
        masks[2] = jnp.where(in_b, 0.0, 1.0).astype(bf16)

    rate = rate_of(rates_ref, head)
    parts = []
    for first in range(0, rows, BLOCK):
        span = pl.ds(first, BLOCK)
        keys = silu(k_ref[span, :]).astype(f32)
        values = silu(v_ref[span, :])
        scaled = (keys * jnp.exp(gap[span, :] * -rate)).astype(bf16)
        spread = jnp.concatenate([values * masks[x, span, :] for x in range(SEGS)], axis=1)
        parts.append(
            lax.dot_general(
                scaled, spread, (((0,), (0,)), ((), ())), preferred_element_type=f32
            )
        )
    early, late = parts
    at_mid = (end_a < BLOCK - 1).astype(jnp.int32) + (end_b < BLOCK - 1).astype(jnp.int32)
    mid = jnp.zeros((E, E), f32)
    for x, end in enumerate((end_a, end_b, jnp.int32(ABSENT))):
        reach = jnp.maximum(jnp.minimum(end, rows - 1) - (BLOCK - 1), 0).astype(f32)
        cols = slice(x * E, (x + 1) * E)
        total = early[:, cols] * scalar_exp(reach * -rate) + late[:, cols]
        sums_ref[:, x] = total.astype(bf16).reshape(sums_ref.shape[0], -1, E)
        mid += early[:, cols] * (at_mid == x).astype(f32)
    mid_ref[0] = mid


def scan_kernel(rows, starts_ref, slots_ref, rates_ref, got_ref, back_ref, counts, carried):
    ranks = got_ref.shape[0]
    count = starts_ref.shape[0]
    stream = rows * ranks
    me = lax.axis_index("ctx")
    rate = rate_of(rates_ref, me * rates_ref.shape[0] // ranks)
    piece = got_ref.shape[2]
    for p in range(ranks):
        counts[p] = 0
    ends = [
        starts_ref[r + 1] - 1 if r + 1 < count else jnp.int32(stream - 1) for r in range(count)
    ]
    homes = [end // rows for end in ends]
    for r in range(count):
        counts[homes[r]] = counts[homes[r]] + 1
    whole = scalar_exp(float(rows) * -rate)
    state = jnp.zeros((piece, E), f32)
    for p in range(ranks):
        carried[p] = state
        back_ref[p, 0] = state.astype(bf16)
        ended = counts[p]
        state = got_ref[p, ended].astype(f32) + state * (whole * (ended == 0).astype(f32))
    for r in range(count):
        second = homes[r] == homes[r - 1] if r else jnp.bool_(False)
        lead = scalar_exp((ends[r] - homes[r] * rows + 1).astype(f32) * -rate)
        lead = lead * jnp.where(second, 0.0, 1.0)
        final = got_ref[homes[r], second.astype(jnp.int32)].astype(f32) + carried[homes[r]] * lead
        back_ref[slots_ref[r], 1] = final.astype(bf16)


def inner_kernel(rows, ranks, starts_ref, rates_ref, q_ref, k_ref, v_ref, inner_ref, act_ref, dist):
    head = pl.program_id(0)

    @pl.when(head == 0)
    def _():
        end_a, end_b = local_ends(starts_ref, rows, ranks)
        for block in range(rows // BLOCK):
            t = lax.broadcasted_iota(jnp.int32, (BLOCK, BLOCK), 0)
            s = lax.broadcasted_iota(jnp.int32, (BLOCK, BLOCK), 1)
            here = t + block * BLOCK
            begin = jnp.where(here <= end_a, 0, jnp.where(here <= end_b, end_a + 1, end_b + 1))
            keep = (s <= t) & (s + block * BLOCK >= begin)
            dist[block] = jnp.where(keep, (t - s).astype(f32), FAR)

    rate = rate_of(rates_ref, head)
    queries = silu(q_ref[...])
    act_ref[...] = queries
    keys = silu(k_ref[...])
    values = silu(v_ref[...])
    for block in range(rows // BLOCK):
        base = block * BLOCK
        for top in range(0, BLOCK, TILE):
            wide = top + TILE
            scores = lax.dot_general(
                queries[base + top : base + top + TILE],
                keys[base : base + wide],
                (((1,), (1,)), ((), ())),
                preferred_element_type=f32,
            )
            decay = jnp.exp(dist[block, top : top + TILE, :wide] * -rate)
            weights = (scores * decay).astype(bf16)
            inner_ref[base + top : base + top + TILE, :] = jnp.dot(
                weights, values[base : base + wide], preferred_element_type=f32
            )


def outer_kernel(
    rows, ranks, starts_ref, rates_ref, back_ref, mid_ref, act_ref, inner_ref,
    out_ref, final_ref, squares_ref, total,
):
    head = pl.program_id(0)
    rate = rate_of(rates_ref, head)
    end_a, end_b = local_ends(starts_ref, rows, ranks)
    incoming = back_ref[:, 0].reshape(E, E)
    final_ref[0, 0] = back_ref[:, 1].reshape(E, E)
    mid_end = jnp.where(end_a >= BLOCK - 1, end_a, jnp.where(end_b >= BLOCK - 1, end_b, ABSENT))
    from_before = (end_a >= BLOCK - 1).astype(f32)
    later = mid_ref[0] + incoming.astype(f32) * (scalar_exp(float(BLOCK) * -rate) * from_before)
    steps = lax.broadcasted_iota(jnp.int32, (BLOCK, E), 0)
    reach = jnp.exp((steps + 1).astype(f32) * -rate)
    for block, (state, last) in enumerate(((incoming, end_a), (later.astype(bf16), mid_end))):
        span = pl.ds(block * BLOCK, BLOCK)
        outer = jnp.dot(act_ref[span, :], state, preferred_element_type=f32)
        lead = jnp.where(steps + block * BLOCK <= last, reach, 0.0)
        attended = inner_ref[span, :] + outer * lead
        out_ref[span, :] = attended
        square = attended * attended

        @pl.when(head == 0)
        def _():
            total[span, :] = square

        @pl.when(head > 0)
        def _():
            total[span, :] += square

    @pl.when(head == pl.num_programs(0) - 1)
    def _():
        pieces = [
            jnp.sum(total[first : first + E, :].T, axis=0, keepdims=True)
            for first in range(0, rows, E)
        ]
        squares_ref[...] = jnp.broadcast_to(
            jnp.concatenate(pieces, axis=0)[None], squares_ref.shape
        )


def norm_kernel(features, squares_ref, gain_ref, att_ref, gate_ref, out_ref):
    row = pl.program_id(0)
    total = jnp.sum(squares_ref[:, pl.ds(row, 1), :], axis=0)
    scale = lax.rsqrt(total * (1.0 / features) + norm_eps)
    column = jnp.broadcast_to(scale, (E, E)).T
    for first in range(0, att_ref.shape[1], E):
        cols = slice(first, first + E)
        gate = 0.5 + 0.5 * jnp.tanh(0.5 * gate_ref[:, cols].astype(f32))
        out_ref[:, cols] = (att_ref[:, cols] * column * gain_ref[:, cols] * gate).astype(bf16)


def cost(flops, moved, hard):
    return pl.CostEstimate(flops=int(flops), bytes_accessed=int(moved), transcendentals=int(hard))


def per_device(
    query, key_in, value_in, gate_in, norm_gain, decay_rate, request_starts, request_slots
):
    rows, width = query.shape
    heads = decay_rate.shape[0]
    ranks = lax.axis_size("ctx")
    groups = lax.axis_size("head")
    per_head = ranks // heads
    piece = E // per_head
    column = pl.BlockSpec((rows, E), lambda h: (0, h))
    params = functools.partial(pltpu.CompilerParams, dimension_semantics=("arbitrary",))

    sums, mid = pl.pallas_call(
        functools.partial(states_kernel, rows, ranks),
        grid=(heads,),
        out_shape=(
            jax.ShapeDtypeStruct((ranks, SEGS, piece, E), bf16),
            jax.ShapeDtypeStruct((heads, E, E), f32),
        ),
        in_specs=[SMEM, SMEM, column, column],
        out_specs=(
            pl.BlockSpec((per_head, SEGS, piece, E), lambda h: (h, 0, 0, 0)),
            pl.BlockSpec((1, E, E), lambda h: (h, 0, 0)),
        ),
        scratch_shapes=[pltpu.VMEM((rows, E), f32), pltpu.VMEM((SEGS, rows, E), bf16)],
        compiler_params=params(vmem_limit_bytes=16 * MIB),
        cost_estimate=cost(2 * rows * width * E * SEGS, 5 * MIB, 3 * rows * width),
        name="states",
    )(request_starts, decay_rate, key_in, value_in)

    got = lax.all_to_all(sums, "ctx", split_axis=0, concat_axis=0, tiled=True)

    inner, act = pl.pallas_call(
        functools.partial(inner_kernel, rows, ranks),
        grid=(heads,),
        out_shape=(
            jax.ShapeDtypeStruct((rows, width), f32),
            jax.ShapeDtypeStruct((rows, width), bf16),
        ),
        in_specs=[SMEM, SMEM, column, column, column],
        out_specs=(column, column),
        scratch_shapes=[pltpu.VMEM((rows // BLOCK, BLOCK, BLOCK), f32)],
        compiler_params=params(vmem_limit_bytes=24 * MIB),
        cost_estimate=cost(4 * rows * width * BLOCK, 12 * MIB, rows * width * 8),
        name="inner",
    )(request_starts, decay_rate, query, key_in, value_in)

    back = pl.pallas_call(
        functools.partial(scan_kernel, rows),
        out_shape=jax.ShapeDtypeStruct((ranks, 2, piece, E), bf16),
        in_specs=[SMEM, SMEM, SMEM, pl.BlockSpec(memory_space=pltpu.VMEM)],
        out_specs=pl.BlockSpec(memory_space=pltpu.VMEM),
        scratch_shapes=[pltpu.SMEM((ranks,), jnp.int32), pltpu.VMEM((ranks, piece, E), f32)],
        compiler_params=pltpu.CompilerParams(vmem_limit_bytes=8 * MIB),
        cost_estimate=cost(MIB, 2 * MIB, 0),
        name="scan",
    )(request_starts, request_slots, decay_rate, got)

    ret = lax.all_to_all(back, "ctx", split_axis=0, concat_axis=0, tiled=True)

    attended, finals, squares = pl.pallas_call(
        functools.partial(outer_kernel, rows, ranks),
        grid=(heads,),
        out_shape=(
            jax.ShapeDtypeStruct((rows, width), f32),
            jax.ShapeDtypeStruct((1, heads, E, E), bf16),
            jax.ShapeDtypeStruct((groups, rows // E, E), f32),
        ),
        in_specs=[
            SMEM,
            SMEM,
            pl.BlockSpec((per_head, 2, piece, E), lambda h: (h, 0, 0, 0)),
            pl.BlockSpec((1, E, E), lambda h: (h, 0, 0)),
            column,
            column,
        ],
        out_specs=(
            column,
            pl.BlockSpec((1, 1, E, E), lambda h: (0, h, 0, 0)),
            pl.BlockSpec((groups, rows // E, E), lambda h: (0, 0, 0)),
        ),
        scratch_shapes=[pltpu.VMEM((rows, E), f32)],
        compiler_params=params(vmem_limit_bytes=16 * MIB),
        cost_estimate=cost(2 * rows * width * E, 10 * MIB, MIB),
        name="outer",
    )(request_starts, decay_rate, ret, mid, act, inner)

    shared = lax.all_to_all(squares, "head", split_axis=0, concat_axis=0, tiled=True)

    band = pl.BlockSpec((E, width), lambda i: (i, 0))
    normed_output = pl.pallas_call(
        functools.partial(norm_kernel, float(width * groups)),
        grid=(rows // E,),
        out_shape=jax.ShapeDtypeStruct((rows, width), bf16),
        in_specs=[
            pl.BlockSpec((groups, rows // E, E), lambda i: (0, 0, 0)),
            pl.BlockSpec((1, width), lambda i: (0, 0)),
            band,
            band,
        ],
        out_specs=band,
        compiler_params=params(vmem_limit_bytes=16 * MIB),
        cost_estimate=cost(6 * rows * width, 8 * MIB, rows * width),
        name="norm",
    )(shared, norm_gain.reshape(1, width), attended, gate_in)
    return (normed_output, finals)


def solution(mesh):
    placed = (
        P("ctx", "head"),
        P("ctx", "head"),
        P("ctx", "head"),
        P("ctx", "head"),
        P("head"),
        P("head"),
        P(),
        P(),
    )
    return jax.shard_map(
        per_device,
        mesh=mesh,
        in_specs=placed,
        out_specs=(P("ctx", "head"), P("ctx", "head", None, None)),
        check_vma=False,
    )
```

```python
import functools

import jax
import jax.numpy as jnp
from jax import lax
from jax.experimental import pallas as pl
from jax.experimental.pallas import tpu as pltpu
from jax.sharding import PartitionSpec as P

E = 128
ENDS_MOST = 2
SEGS = ENDS_MOST + 1
BLOCK = 512
TILE = 256
ABSENT = 1 << 20
FAR = 1e38
LOG2E = 1.4426950408889634
norm_eps = 1e-06
MIB = 1 << 20
LIMIT = 62 * MIB
ROOM = 44 * MIB
f32 = jnp.float32
bf16 = jnp.bfloat16
SMEM = pl.BlockSpec(memory_space=pltpu.SMEM)
VMEM = pl.BlockSpec(memory_space=pltpu.VMEM)
HBM = pl.BlockSpec(memory_space=pltpu.HBM)


def silu(values):
    half = values.astype(f32) * 0.5
    return (half + half * jnp.tanh(half)).astype(bf16)


def rate_of(rates_ref, head):
    return jnp.maximum(rates_ref[head], 1e-30)


def end_of(starts_ref, request, stream):
    count = starts_ref.shape[0]
    following = starts_ref[jnp.minimum(request + 1, count - 1)]
    return jnp.where(request < count - 1, following - 1, stream - 1)


def local_ends(starts_ref, rows, ranks):
    stream = rows * ranks
    offset = lax.axis_index("ctx") * rows
    count = starts_ref.shape[0]
    first = jnp.int32(0)
    for request in range(count - 1):
        first += (starts_ref[request + 1] - 1 < offset).astype(jnp.int32)
    end_a = end_of(starts_ref, first, stream) - offset
    end_b = end_of(starts_ref, first + 1, stream) - offset
    end_b = jnp.where(first + 1 < count, end_b, ABSENT)
    return end_a, end_b


def power_of(rates_ref, head):
    return rate_of(rates_ref, head) * -LOG2E


def scalar_exp2(value):
    return jnp.exp2(jnp.full((1, E), value, f32))


def scalar_exp(value):
    return jnp.exp(jnp.full((1, E), value, f32))


def lanes(head):
    return pl.ds(pl.multiple_of(head * E, E), E)


def states_kernel(
    rows, ranks, starts_hbm, rates_hbm, k_hbm, v_hbm, sums_hbm, mid_hbm,
    starts_ref, rates_ref, k_raw, v_raw, gap, masks, sums, mids, sems, arrived, left,
):
    heads = k_raw.shape[1] // E
    small = (
        pltpu.make_async_copy(starts_hbm, starts_ref, sems.at[0]),
        pltpu.make_async_copy(rates_hbm, rates_ref, sems.at[1]),
    )

    def load(head):
        at = lanes(head)
        return (
            pltpu.make_async_copy(k_hbm.at[:, at], k_raw.at[:, at], arrived.at[0, head]),
            pltpu.make_async_copy(v_hbm.at[:, at], v_raw.at[:, at], arrived.at[1, head]),
        )

    share = sums.shape[0] // heads

    def store(head):
        pieces = pl.ds(head * share, share)
        return (
            pltpu.make_async_copy(sums.at[pieces], sums_hbm.at[pieces], left.at[0, head]),
            pltpu.make_async_copy(mids.at[head], mid_hbm.at[head], left.at[1, head]),
        )

    for copy in small:
        copy.start()
    for head in range(heads):
        for copy in load(head):
            copy.start()
    for copy in small:
        copy.wait()
    end_a, end_b = local_ends(starts_ref, rows, ranks)
    token = lax.broadcasted_iota(jnp.int32, (rows, E), 0)
    in_a = token <= end_a
    in_b = token <= end_b
    seg_end = jnp.where(in_a, end_a, jnp.where(in_b, end_b, ABSENT))
    block_end = (token // BLOCK) * BLOCK + (BLOCK - 1)
    gap[...] = (jnp.minimum(seg_end, block_end) - token).astype(f32)
    masks[0] = jnp.where(in_a, 1.0, 0.0).astype(bf16)
    masks[1] = jnp.where(in_b, jnp.where(in_a, 0.0, 1.0), 0.0).astype(bf16)
    masks[2] = jnp.where(in_b, 0.0, 1.0).astype(bf16)
    at_mid = (end_a < BLOCK - 1).astype(jnp.int32) + (end_b < BLOCK - 1).astype(jnp.int32)

    @pl.loop(0, heads)
    def _(head):
        at = lanes(head)
        power = power_of(rates_ref, head)
        for copy in load(head):
            copy.wait()
        parts = []
        for first in range(0, rows, BLOCK):
            span = pl.ds(first, BLOCK)
            keys = silu(k_raw[span, at])
            values = silu(v_raw[span, at])
            scaled = (keys.astype(f32) * jnp.exp2(gap[span, :] * power)).astype(bf16)
            spread = jnp.concatenate([values * masks[x, span, :] for x in range(SEGS)], axis=1)
            parts.append(
                lax.dot_general(
                    scaled, spread, (((0,), (0,)), ((), ())), preferred_element_type=f32
                )
            )
        early, late = parts
        mid = jnp.zeros((E, E), f32)
        for x, end in enumerate((end_a, end_b, jnp.int32(ABSENT))):
            reach = jnp.maximum(jnp.minimum(end, rows - 1) - (BLOCK - 1), 0).astype(f32)
            cols = slice(x * E, (x + 1) * E)
            total = early[:, cols] * scalar_exp2(reach * power) + late[:, cols]
            sums[pl.ds(head * share, share), x] = total.astype(bf16).reshape(share, -1, E)
            mid += early[:, cols] * (at_mid == x).astype(f32)
        mids[head] = mid
        for copy in store(head):
            copy.start()

    for head in range(heads):
        for copy in store(head):
            copy.wait()


def request_ends(starts_ref, rows, ranks):
    count = starts_ref.shape[0]
    ends = [
        starts_ref[r + 1] - 1 if r + 1 < count else jnp.int32(rows * ranks - 1)
        for r in range(count)
    ]
    return ends, [end // rows for end in ends]


def advance(rows, rate, homes, got_ref, counts, keep):
    ranks = got_ref.shape[0]
    for p in range(ranks):
        counts[p] = 0
    for home in homes:
        counts[home] = counts[home] + 1
    whole = scalar_exp(float(rows) * -rate)
    state = jnp.zeros(got_ref.shape[2:], f32)
    for p in range(ranks):
        keep(p, state)
        ended = counts[p]
        state = got_ref[p, ended].astype(f32) + state * (whole * (ended == 0).astype(f32))


def my_rate(rates_ref, ranks):
    return rate_of(rates_ref, lax.axis_index("ctx") * rates_ref.shape[0] // ranks)


def scan_kernel(
    rows, starts_ref, slots_ref, rates_ref, got_ref, back_ref, counts, carried
):
    ranks = got_ref.shape[0]
    rate = my_rate(rates_ref, ranks)
    ends, homes = request_ends(starts_ref, rows, ranks)

    def keep(p, state):
        carried[p] = state
        back_ref[p, 0] = state.astype(bf16)

    advance(rows, rate, homes, got_ref, counts, keep)
    for r, (end, home) in enumerate(zip(ends, homes)):
        second = home == homes[r - 1] if r else jnp.bool_(False)
        lead = scalar_exp((end - home * rows + 1).astype(f32) * -rate)
        lead = lead * jnp.where(second, 0.0, 1.0)
        final = got_ref[home, second.astype(jnp.int32)].astype(f32) + carried[home] * lead
        back_ref[slots_ref[r], 1] = final.astype(bf16)


def inner_kernel(
    rows, ranks, starts_ref, rates_ref, q_hbm, k_hbm, v_hbm, inner_hbm, act_hbm,
    q_raw, k_raw, v_raw, inner, act, dist, arrived, left,
):
    heads = q_raw.shape[1] // E

    def load(head):
        at = lanes(head)
        return (
            pltpu.make_async_copy(q_hbm.at[:, at], q_raw.at[:, at], arrived.at[0, head]),
            pltpu.make_async_copy(k_hbm.at[:, at], k_raw.at[:, at], arrived.at[1, head]),
            pltpu.make_async_copy(v_hbm.at[:, at], v_raw.at[:, at], arrived.at[2, head]),
        )

    def store(head):
        at = lanes(head)
        return (
            pltpu.make_async_copy(inner.at[:, at], inner_hbm.at[:, at], left.at[0, head]),
            pltpu.make_async_copy(act.at[:, at], act_hbm.at[:, at], left.at[1, head]),
        )

    for head in range(heads):
        for copy in load(head):
            copy.start()
    end_a, end_b = local_ends(starts_ref, rows, ranks)
    for block in range(rows // BLOCK):
        t = lax.broadcasted_iota(jnp.int32, (BLOCK, BLOCK), 0)
        s = lax.broadcasted_iota(jnp.int32, (BLOCK, BLOCK), 1)
        here = t + block * BLOCK
        begin = jnp.where(here <= end_a, 0, jnp.where(here <= end_b, end_a + 1, end_b + 1))
        keep = (s <= t) & (s + block * BLOCK >= begin)
        dist[block] = jnp.where(keep, (t - s).astype(f32), FAR)

    @pl.loop(0, heads)
    def _(head):
        at = lanes(head)
        power = power_of(rates_ref, head)
        for copy in load(head):
            copy.wait()
        act[:, at] = silu(q_raw[:, at])
        keys = silu(k_raw[:, at])
        values = silu(v_raw[:, at])
        for block in range(rows // BLOCK):
            base = block * BLOCK
            for top in range(0, BLOCK, TILE):
                wide = top + TILE
                mine = pl.ds(base + top, TILE)
                scores = lax.dot_general(
                    act[mine, at],
                    keys[base : base + wide],
                    (((1,), (1,)), ((), ())),
                    preferred_element_type=f32,
                )
                decay = jnp.exp2(dist[block, top : top + TILE, :wide] * power)
                weights = (scores * decay).astype(bf16)
                inner[mine, at] = jnp.dot(
                    weights, values[base : base + wide], preferred_element_type=f32
                )
        for copy in store(head):
            copy.start()

    for head in range(heads):
        for copy in store(head):
            copy.wait()


def outer_kernel(
    rows, ranks, starts_hbm, rates_hbm, back_hbm, mid_hbm, act_hbm, inner_hbm,
    out_ref, final_hbm, squares_ref,
    starts_ref, rates_ref, back, mid, act, inner, total, arrived, left,
):
    heads = mid.shape[0]
    share = back.shape[0] // heads

    def load(head):
        at = lanes(head)
        return (
            pltpu.make_async_copy(act_hbm.at[:, at], act.at[:, at], arrived.at[0, head]),
            pltpu.make_async_copy(inner_hbm.at[:, at], inner.at[:, at], arrived.at[1, head]),
        )

    whole = (
        pltpu.make_async_copy(starts_hbm, starts_ref, arrived.at[0, heads + 1]),
        pltpu.make_async_copy(rates_hbm, rates_ref, arrived.at[1, heads + 1]),
        pltpu.make_async_copy(back_hbm, back, arrived.at[0, heads]),
        pltpu.make_async_copy(mid_hbm, mid, arrived.at[1, heads]),
    )
    finals = pltpu.make_async_copy(back.at[:, 1], final_hbm, left.at[0])
    for copy in whole:
        copy.start()
    for head in range(heads):
        for copy in load(head):
            copy.start()
    for copy in whole:
        copy.wait()
    finals.start()
    end_a, end_b = local_ends(starts_ref, rows, ranks)
    mid_end = jnp.where(end_a >= BLOCK - 1, end_a, jnp.where(end_b >= BLOCK - 1, end_b, ABSENT))
    from_before = (end_a >= BLOCK - 1).astype(f32)
    total[...] = jnp.zeros_like(total)

    @pl.loop(0, heads)
    def _(head):
        at = lanes(head)
        power = power_of(rates_ref, head)
        incoming = back[pl.ds(head * share, share), 0].reshape(E, E)
        later = mid[head] + incoming.astype(f32) * (scalar_exp2(float(BLOCK) * power) * from_before)
        steps = lax.broadcasted_iota(jnp.int32, (BLOCK, E), 0)
        reach = jnp.exp2((steps + 1).astype(f32) * power)
        for copy in load(head):
            copy.wait()
        for block, (state, last) in enumerate(((incoming, end_a), (later.astype(bf16), mid_end))):
            span = pl.ds(block * BLOCK, BLOCK)
            outer = jnp.dot(act[span, at], state, preferred_element_type=f32)
            lead = jnp.where(steps + block * BLOCK <= last, reach, 0.0)
            attended = inner[span, at] + outer * lead
            out_ref[span, at] = attended
            total[span, :] += attended * attended

    row_sums = jnp.concatenate(
        [
            jnp.sum(total[first : first + E, :].T, axis=0, keepdims=True)
            for first in range(0, rows, E)
        ],
        axis=0,
    )
    squares_ref[...] = jnp.broadcast_to(row_sums[None], squares_ref.shape)
    finals.wait()


def norm_kernel(
    features, squares_ref, gain_ref, att_ref, gate_hbm, out_hbm, gate, out, sems
):
    bands = out.shape[0] // E

    def load(band):
        span = pl.ds(band * E, E)
        return pltpu.make_async_copy(gate_hbm.at[span, :], gate.at[span, :], sems.at[0, band])

    def store(band):
        span = pl.ds(band * E, E)
        return pltpu.make_async_copy(out.at[span, :], out_hbm.at[span, :], sems.at[1, band])

    for band in range(bands):
        load(band).start()
    total = jnp.sum(squares_ref[...], axis=0)
    scale = lax.rsqrt(total * (1.0 / features) + norm_eps)
    for band in range(bands):
        span = pl.ds(band * E, E)
        column = jnp.broadcast_to(scale[band : band + 1], (E, E)).T
        load(band).wait()
        for first in range(0, out.shape[1], E):
            cols = slice(first, first + E)
            opened = 0.5 + 0.5 * jnp.tanh(0.5 * gate[span, cols].astype(f32))
            scaled = att_ref[span, cols] * column * gain_ref[:, cols]
            out[span, cols] = (scaled * opened).astype(bf16)
        store(band).start()
    for band in range(bands):
        store(band).wait()


def cost(flops, moved, hard):
    return pl.CostEstimate(flops=int(flops), bytes_accessed=int(moved), transcendentals=int(hard))


def swap(array, axis):
    return lax.all_to_all(array, axis, split_axis=0, concat_axis=0, tiled=True)


def per_device(
    query, key_in, value_in, gate_in, norm_gain, decay_rate, request_starts, request_slots
):
    return local(
        lax.axis_size("ctx"), lax.axis_size("head"), query, key_in, value_in, gate_in, norm_gain,
        decay_rate, request_starts, request_slots,
    )


def local(
    ranks, groups, query, key_in, value_in, gate_in, norm_gain, decay_rate, request_starts,
    request_slots,
):
    rows, width = query.shape
    heads = decay_rate.shape[0]
    piece = E * heads // ranks

    sums, mid = pl.pallas_call(
        functools.partial(states_kernel, rows, ranks),
        out_shape=(
            jax.ShapeDtypeStruct((ranks, SEGS, piece, E), bf16),
            jax.ShapeDtypeStruct((heads, E, E), f32),
        ),
        in_specs=[HBM, HBM, HBM, HBM],
        out_specs=(HBM, HBM),
        scratch_shapes=[
            pltpu.SMEM(request_starts.shape, jnp.int32),
            pltpu.SMEM(decay_rate.shape, f32),
            pltpu.VMEM((rows, width), bf16),
            pltpu.VMEM((rows, width), bf16),
            pltpu.VMEM((rows, E), f32),
            pltpu.VMEM((SEGS, rows, E), bf16),
            pltpu.VMEM((ranks, SEGS, piece, E), bf16),
            pltpu.VMEM((heads, E, E), f32),
            pltpu.SemaphoreType.DMA((2,)),
            pltpu.SemaphoreType.DMA((2, heads)),
            pltpu.SemaphoreType.DMA((2, heads)),
        ],
        compiler_params=pltpu.CompilerParams(vmem_limit_bytes=LIMIT),
        cost_estimate=cost(2 * rows * width * E * SEGS, 5 * MIB, 3 * rows * width),
        name="states",
    )(request_starts, decay_rate, key_in, value_in)

    got = swap(sums, "ctx")

    inner, act = pl.pallas_call(
        functools.partial(inner_kernel, rows, ranks),
        out_shape=(
            jax.ShapeDtypeStruct((rows, width), f32),
            jax.ShapeDtypeStruct((rows, width), bf16),
        ),
        in_specs=[SMEM, SMEM, HBM, HBM, HBM],
        out_specs=(HBM, HBM),
        scratch_shapes=[
            pltpu.VMEM((rows, width), bf16),
            pltpu.VMEM((rows, width), bf16),
            pltpu.VMEM((rows, width), bf16),
            pltpu.VMEM((rows, width), f32),
            pltpu.VMEM((rows, width), bf16),
            pltpu.VMEM((rows // BLOCK, BLOCK, BLOCK), f32),
            pltpu.SemaphoreType.DMA((3, heads)),
            pltpu.SemaphoreType.DMA((2, heads)),
        ],
        compiler_params=pltpu.CompilerParams(vmem_limit_bytes=LIMIT),
        cost_estimate=cost(4 * rows * width * BLOCK, 12 * rows * width, rows * width * 8),
        name="inner",
    )(request_starts, decay_rate, query, key_in, value_in)

    back = pl.pallas_call(
        functools.partial(scan_kernel, rows),
        out_shape=jax.ShapeDtypeStruct((ranks, 2, piece, E), bf16),
        in_specs=[SMEM, SMEM, SMEM, VMEM],
        out_specs=VMEM,
        scratch_shapes=[pltpu.SMEM((ranks,), jnp.int32), pltpu.VMEM((ranks, piece, E), f32)],
        compiler_params=pltpu.CompilerParams(vmem_limit_bytes=8 * MIB),
        cost_estimate=cost(MIB, 2 * MIB, 0),
        name="scan",
    )(request_starts, request_slots, decay_rate, got)

    returned = swap(back, "ctx")

    attended, final_states, squares = pl.pallas_call(
        functools.partial(outer_kernel, rows, ranks),
        out_shape=(
            jax.ShapeDtypeStruct((rows, width), f32),
            jax.ShapeDtypeStruct((ranks, piece, E), bf16),
            jax.ShapeDtypeStruct((groups, rows // E, E), f32),
        ),
        in_specs=[HBM] * 6,
        out_specs=(VMEM, HBM, VMEM),
        scratch_shapes=[
            pltpu.SMEM(request_starts.shape, jnp.int32),
            pltpu.SMEM(decay_rate.shape, f32),
            pltpu.VMEM((ranks, 2, piece, E), bf16),
            pltpu.VMEM((heads, E, E), f32),
            pltpu.VMEM((rows, width), bf16),
            pltpu.VMEM((rows, width), f32),
            pltpu.VMEM((rows, E), f32),
            pltpu.SemaphoreType.DMA((2, heads + 2)),
            pltpu.SemaphoreType.DMA((1,)),
        ],
        compiler_params=pltpu.CompilerParams(vmem_limit_bytes=ROOM),
        cost_estimate=cost(2 * rows * width * E, 10 * MIB, MIB),
        name="outer",
    )(request_starts, decay_rate, returned, mid, act, inner)

    shared = swap(squares, "head")

    normed_output = pl.pallas_call(
        functools.partial(norm_kernel, float(width * groups)),
        out_shape=jax.ShapeDtypeStruct((rows, width), bf16),
        in_specs=[VMEM, VMEM, VMEM, HBM],
        out_specs=HBM,
        scratch_shapes=[
            pltpu.VMEM((rows, width), bf16),
            pltpu.VMEM((rows, width), bf16),
            pltpu.SemaphoreType.DMA((2, rows // E)),
        ],
        compiler_params=pltpu.CompilerParams(vmem_limit_bytes=ROOM),
        cost_estimate=cost(6 * rows * width, 8 * MIB, rows * width),
        name="norm",
    )(shared, norm_gain.reshape(1, width), attended, gate_in)
    return (normed_output, final_states.reshape(1, heads, E, E))


def solution(mesh):
    placed = (
        P("ctx", "head"),
        P("ctx", "head"),
        P("ctx", "head"),
        P("ctx", "head"),
        P("head"),
        P("head"),
        P(),
        P(),
    )
    return jax.shard_map(
        per_device,
        mesh=mesh,
        in_specs=placed,
        out_specs=(P("ctx", "head"), P("ctx", "head", None, None)),
        check_vma=False,
    )
```

```python
import functools

import jax
import jax.numpy as jnp
from jax import lax
from jax.experimental import pallas as pl
from jax.experimental.pallas import tpu as pltpu
from jax.sharding import PartitionSpec as P

E = 128
ENDS_MOST = 2
SEGS = ENDS_MOST + 1
BLOCK = 512
TILE = 256
ABSENT = 1 << 20
FAR = 1e38
LOG2E = 1.4426950408889634
norm_eps = 1e-06
MIB = 1 << 20
LIMIT = 62 * MIB
ROOM = 40 * MIB
f32 = jnp.float32
bf16 = jnp.bfloat16
SMEM = pl.BlockSpec(memory_space=pltpu.SMEM)
VMEM = pl.BlockSpec(memory_space=pltpu.VMEM)
HBM = pl.BlockSpec(memory_space=pltpu.HBM)


def silu(values):
    half = values.astype(f32) * 0.5
    return (half + half * jnp.tanh(half)).astype(bf16)


def rate_of(rates_ref, head):
    return jnp.maximum(rates_ref[head], 1e-30)


def end_of(starts_ref, request, stream):
    count = starts_ref.shape[0]
    following = starts_ref[jnp.minimum(request + 1, count - 1)]
    return jnp.where(request < count - 1, following - 1, stream - 1)


def local_ends(starts_ref, rows, ranks):
    stream = rows * ranks
    offset = lax.axis_index("ctx") * rows
    count = starts_ref.shape[0]
    first = jnp.int32(0)
    for request in range(count - 1):
        first += (starts_ref[request + 1] - 1 < offset).astype(jnp.int32)
    end_a = end_of(starts_ref, first, stream) - offset
    end_b = end_of(starts_ref, first + 1, stream) - offset
    end_b = jnp.where(first + 1 < count, end_b, ABSENT)
    return end_a, end_b


def power_of(rates_ref, head):
    return rate_of(rates_ref, head) * -LOG2E


def scalar_exp2(value):
    return jnp.exp2(jnp.full((1, E), value, f32))


def scalar_exp(value):
    return jnp.exp(jnp.full((1, E), value, f32))


def lanes(head):
    return pl.ds(pl.multiple_of(head * E, E), E)


def states_kernel(
    rows, ranks, starts_hbm, rates_hbm, k_hbm, v_hbm, sums_hbm, mid_hbm,
    starts_ref, rates_ref, k_raw, v_raw, gap, masks, sums, mids, sems, arrived, left,
):
    heads = k_raw.shape[1] // E
    small = (
        pltpu.make_async_copy(starts_hbm, starts_ref, sems.at[0]),
        pltpu.make_async_copy(rates_hbm, rates_ref, sems.at[1]),
    )

    def load(head):
        at = lanes(head)
        return (
            pltpu.make_async_copy(k_hbm.at[:, at], k_raw.at[:, at], arrived.at[0, head]),
            pltpu.make_async_copy(v_hbm.at[:, at], v_raw.at[:, at], arrived.at[1, head]),
        )

    share = sums.shape[0] // heads

    def store(head):
        pieces = pl.ds(head * share, share)
        return (
            pltpu.make_async_copy(sums.at[pieces], sums_hbm.at[pieces], left.at[0, head]),
            pltpu.make_async_copy(mids.at[head], mid_hbm.at[head], left.at[1, head]),
        )

    for copy in small:
        copy.start()
    for head in range(heads):
        for copy in load(head):
            copy.start()
    for copy in small:
        copy.wait()
    end_a, end_b = local_ends(starts_ref, rows, ranks)
    token = lax.broadcasted_iota(jnp.int32, (rows, E), 0)
    in_a = token <= end_a
    in_b = token <= end_b
    seg_end = jnp.where(in_a, end_a, jnp.where(in_b, end_b, ABSENT))
    block_end = (token // BLOCK) * BLOCK + (BLOCK - 1)
    gap[...] = (jnp.minimum(seg_end, block_end) - token).astype(f32)
    masks[0] = jnp.where(in_a, 1.0, 0.0).astype(bf16)
    masks[1] = jnp.where(in_b, jnp.where(in_a, 0.0, 1.0), 0.0).astype(bf16)
    masks[2] = jnp.where(in_b, 0.0, 1.0).astype(bf16)
    at_mid = (end_a < BLOCK - 1).astype(jnp.int32) + (end_b < BLOCK - 1).astype(jnp.int32)

    @pl.loop(0, heads)
    def _(head):
        at = lanes(head)
        power = power_of(rates_ref, head)
        for copy in load(head):
            copy.wait()
        parts = []
        for first in range(0, rows, BLOCK):
            span = pl.ds(first, BLOCK)
            keys = silu(k_raw[span, at])
            values = silu(v_raw[span, at])
            scaled = (keys.astype(f32) * jnp.exp2(gap[span, :] * power)).astype(bf16)
            spread = jnp.concatenate([values * masks[x, span, :] for x in range(SEGS)], axis=1)
            parts.append(
                lax.dot_general(
                    scaled, spread, (((0,), (0,)), ((), ())), preferred_element_type=f32
                )
            )
        early, late = parts
        mid = jnp.zeros((E, E), f32)
        for x, end in enumerate((end_a, end_b, jnp.int32(ABSENT))):
            reach = jnp.maximum(jnp.minimum(end, rows - 1) - (BLOCK - 1), 0).astype(f32)
            cols = slice(x * E, (x + 1) * E)
            total = early[:, cols] * scalar_exp2(reach * power) + late[:, cols]
            sums[pl.ds(head * share, share), x] = total.astype(bf16).reshape(share, -1, E)
            mid += early[:, cols] * (at_mid == x).astype(f32)
        mids[head] = mid
        for copy in store(head):
            copy.start()

    for head in range(heads):
        for copy in store(head):
            copy.wait()


def request_ends(starts_ref, rows, ranks):
    count = starts_ref.shape[0]
    ends = [
        starts_ref[r + 1] - 1 if r + 1 < count else jnp.int32(rows * ranks - 1)
        for r in range(count)
    ]
    return ends, [end // rows for end in ends]


def advance(rows, rate, homes, got_ref, counts, keep):
    ranks = got_ref.shape[0]
    for p in range(ranks):
        counts[p] = 0
    for home in homes:
        counts[home] = counts[home] + 1
    whole = scalar_exp(float(rows) * -rate)
    state = jnp.zeros(got_ref.shape[2:], f32)
    for p in range(ranks):
        keep(p, state)
        ended = counts[p]
        state = got_ref[p, ended].astype(f32) + state * (whole * (ended == 0).astype(f32))


def my_rate(rates_ref, ranks):
    return rate_of(rates_ref, lax.axis_index("ctx") * rates_ref.shape[0] // ranks)


def scan_kernel(
    rows, starts_ref, slots_ref, rates_ref, got_ref, inner_hbm, back_ref, counts, carried
):
    ranks = got_ref.shape[0]
    rate = my_rate(rates_ref, ranks)
    ends, homes = request_ends(starts_ref, rows, ranks)

    def keep(p, state):
        carried[p] = state
        back_ref[p, 0] = state.astype(bf16)

    advance(rows, rate, homes, got_ref, counts, keep)
    for r, (end, home) in enumerate(zip(ends, homes)):
        second = home == homes[r - 1] if r else jnp.bool_(False)
        lead = scalar_exp((end - home * rows + 1).astype(f32) * -rate)
        lead = lead * jnp.where(second, 0.0, 1.0)
        final = got_ref[home, second.astype(jnp.int32)].astype(f32) + carried[home] * lead
        back_ref[slots_ref[r], 1] = final.astype(bf16)


def inner_kernel(
    rows, ranks, starts_ref, rates_ref, q_hbm, k_hbm, v_hbm, inner_hbm, act_hbm,
    q_raw, k_raw, v_raw, inner, act, dist, arrived, left,
):
    heads = q_raw.shape[1] // E

    def load(head):
        at = lanes(head)
        return (
            pltpu.make_async_copy(q_hbm.at[:, at], q_raw.at[:, at], arrived.at[0, head]),
            pltpu.make_async_copy(k_hbm.at[:, at], k_raw.at[:, at], arrived.at[1, head]),
            pltpu.make_async_copy(v_hbm.at[:, at], v_raw.at[:, at], arrived.at[2, head]),
        )

    def store(head):
        at = lanes(head)
        return (
            pltpu.make_async_copy(inner.at[:, at], inner_hbm.at[:, at], left.at[0, head]),
            pltpu.make_async_copy(act.at[:, at], act_hbm.at[:, at], left.at[1, head]),
        )

    for head in range(heads):
        for copy in load(head):
            copy.start()
    end_a, end_b = local_ends(starts_ref, rows, ranks)
    for block in range(rows // BLOCK):
        t = lax.broadcasted_iota(jnp.int32, (BLOCK, BLOCK), 0)
        s = lax.broadcasted_iota(jnp.int32, (BLOCK, BLOCK), 1)
        here = t + block * BLOCK
        begin = jnp.where(here <= end_a, 0, jnp.where(here <= end_b, end_a + 1, end_b + 1))
        keep = (s <= t) & (s + block * BLOCK >= begin)
        dist[block] = jnp.where(keep, (t - s).astype(f32), FAR)

    @pl.loop(0, heads)
    def _(head):
        at = lanes(head)
        power = power_of(rates_ref, head)
        for copy in load(head):
            copy.wait()
        act[:, at] = silu(q_raw[:, at])
        keys = silu(k_raw[:, at])
        values = silu(v_raw[:, at])
        for block in range(rows // BLOCK):
            base = block * BLOCK
            for top in range(0, BLOCK, TILE):
                wide = top + TILE
                mine = pl.ds(base + top, TILE)
                scores = lax.dot_general(
                    act[mine, at],
                    keys[base : base + wide],
                    (((1,), (1,)), ((), ())),
                    preferred_element_type=f32,
                )
                decay = jnp.exp2(dist[block, top : top + TILE, :wide] * power)
                weights = (scores * decay).astype(bf16)
                inner[mine, at] = jnp.dot(
                    weights, values[base : base + wide], preferred_element_type=f32
                )
        for copy in store(head):
            copy.start()

    for head in range(heads):
        for copy in store(head):
            copy.wait()


def outer_kernel(
    rows, ranks, starts_ref, rates_ref, back_ref, mid_ref, act_ref, inner_ref,
    out_ref, final_hbm, squares_ref, total, left,
):
    heads = mid_ref.shape[0]
    share = back_ref.shape[0] // heads
    finals = pltpu.make_async_copy(back_ref.at[:, 1], final_hbm, left.at[0])
    finals.start()
    end_a, end_b = local_ends(starts_ref, rows, ranks)
    mid_end = jnp.where(end_a >= BLOCK - 1, end_a, jnp.where(end_b >= BLOCK - 1, end_b, ABSENT))
    from_before = (end_a >= BLOCK - 1).astype(f32)
    total[...] = jnp.zeros_like(total)

    @pl.loop(0, heads)
    def _(head):
        at = lanes(head)
        power = power_of(rates_ref, head)
        incoming = back_ref[pl.ds(head * share, share), 0].reshape(E, E)
        later = mid_ref[head] + incoming.astype(f32) * (
            scalar_exp2(float(BLOCK) * power) * from_before
        )
        steps = lax.broadcasted_iota(jnp.int32, (BLOCK, E), 0)
        reach = jnp.exp2((steps + 1).astype(f32) * power)
        for block, (state, last) in enumerate(((incoming, end_a), (later.astype(bf16), mid_end))):
            span = pl.ds(block * BLOCK, BLOCK)
            outer = jnp.dot(act_ref[span, at], state, preferred_element_type=f32)
            lead = jnp.where(steps + block * BLOCK <= last, reach, 0.0)
            attended = inner_ref[span, at] + outer * lead
            out_ref[span, at] = attended
            total[span, :] += attended * attended

    row_sums = jnp.concatenate(
        [
            jnp.sum(total[first : first + E, :].T, axis=0, keepdims=True)
            for first in range(0, rows, E)
        ],
        axis=0,
    )
    squares_ref[...] = jnp.broadcast_to(row_sums[None], squares_ref.shape)
    finals.wait()


def norm_kernel(
    features, squares_ref, gain_ref, att_ref, gate_ref, out_hbm, out, sems
):
    bands = out.shape[0] // E

    def store(band):
        span = pl.ds(band * E, E)
        return pltpu.make_async_copy(out.at[span, :], out_hbm.at[span, :], sems.at[band])

    total = jnp.sum(squares_ref[...], axis=0)
    scale = lax.rsqrt(total * (1.0 / features) + norm_eps)
    for band in range(bands):
        span = pl.ds(band * E, E)
        column = jnp.broadcast_to(scale[band : band + 1], (E, E)).T
        for first in range(0, out.shape[1], E):
            cols = slice(first, first + E)
            opened = 0.5 + 0.5 * jnp.tanh(0.5 * gate_ref[span, cols].astype(f32))
            scaled = att_ref[span, cols] * column * gain_ref[:, cols]
            out[span, cols] = (scaled * opened).astype(bf16)
        store(band).start()
    for band in range(bands):
        store(band).wait()


def cost(flops, moved, hard):
    return pl.CostEstimate(flops=int(flops), bytes_accessed=int(moved), transcendentals=int(hard))


def swap(array, axis):
    return lax.all_to_all(array, axis, split_axis=0, concat_axis=0, tiled=True)


def per_device(
    query, key_in, value_in, gate_in, norm_gain, decay_rate, request_starts, request_slots
):
    return local(
        lax.axis_size("ctx"), lax.axis_size("head"), query, key_in, value_in, gate_in, norm_gain,
        decay_rate, request_starts, request_slots,
    )


def local(
    ranks, groups, query, key_in, value_in, gate_in, norm_gain, decay_rate, request_starts,
    request_slots,
):
    rows, width = query.shape
    heads = decay_rate.shape[0]
    piece = E * heads // ranks

    sums, mid = pl.pallas_call(
        functools.partial(states_kernel, rows, ranks),
        out_shape=(
            jax.ShapeDtypeStruct((ranks, SEGS, piece, E), bf16),
            jax.ShapeDtypeStruct((heads, E, E), f32),
        ),
        in_specs=[HBM, HBM, HBM, HBM],
        out_specs=(HBM, HBM),
        scratch_shapes=[
            pltpu.SMEM(request_starts.shape, jnp.int32),
            pltpu.SMEM(decay_rate.shape, f32),
            pltpu.VMEM((rows, width), bf16),
            pltpu.VMEM((rows, width), bf16),
            pltpu.VMEM((rows, E), f32),
            pltpu.VMEM((SEGS, rows, E), bf16),
            pltpu.VMEM((ranks, SEGS, piece, E), bf16),
            pltpu.VMEM((heads, E, E), f32),
            pltpu.SemaphoreType.DMA((2,)),
            pltpu.SemaphoreType.DMA((2, heads)),
            pltpu.SemaphoreType.DMA((2, heads)),
        ],
        compiler_params=pltpu.CompilerParams(vmem_limit_bytes=LIMIT),
        cost_estimate=cost(2 * rows * width * E * SEGS, 5 * MIB, 3 * rows * width),
        name="states",
    )(request_starts, decay_rate, key_in, value_in)

    got = swap(sums, "ctx")

    inner, act = pl.pallas_call(
        functools.partial(inner_kernel, rows, ranks),
        out_shape=(
            jax.ShapeDtypeStruct((rows, width), f32),
            jax.ShapeDtypeStruct((rows, width), bf16),
        ),
        in_specs=[SMEM, SMEM, HBM, HBM, HBM],
        out_specs=(HBM, HBM),
        scratch_shapes=[
            pltpu.VMEM((rows, width), bf16),
            pltpu.VMEM((rows, width), bf16),
            pltpu.VMEM((rows, width), bf16),
            pltpu.VMEM((rows, width), f32),
            pltpu.VMEM((rows, width), bf16),
            pltpu.VMEM((rows // BLOCK, BLOCK, BLOCK), f32),
            pltpu.SemaphoreType.DMA((3, heads)),
            pltpu.SemaphoreType.DMA((2, heads)),
        ],
        compiler_params=pltpu.CompilerParams(vmem_limit_bytes=LIMIT),
        cost_estimate=cost(4 * rows * width * BLOCK, 12 * rows * width, rows * width * 8),
        name="inner",
    )(request_starts, decay_rate, query, key_in, value_in)

    back = pl.pallas_call(
        functools.partial(scan_kernel, rows),
        out_shape=jax.ShapeDtypeStruct((ranks, 2, piece, E), bf16),
        in_specs=[SMEM, SMEM, SMEM, VMEM, HBM],
        out_specs=VMEM,
        scratch_shapes=[pltpu.SMEM((ranks,), jnp.int32), pltpu.VMEM((ranks, piece, E), f32)],
        compiler_params=pltpu.CompilerParams(vmem_limit_bytes=50 * MIB),
        cost_estimate=cost(MIB, 2 * MIB, 0),
        name="scan",
    )(request_starts, request_slots, decay_rate, got, inner)

    returned = swap(back, "ctx")

    attended, final_states, squares = pl.pallas_call(
        functools.partial(outer_kernel, rows, ranks),
        out_shape=(
            jax.ShapeDtypeStruct((rows, width), f32),
            jax.ShapeDtypeStruct((ranks, piece, E), bf16),
            jax.ShapeDtypeStruct((groups, rows // E, E), f32),
        ),
        in_specs=[SMEM, SMEM, VMEM, VMEM, VMEM, VMEM],
        out_specs=(VMEM, HBM, VMEM),
        scratch_shapes=[pltpu.VMEM((rows, E), f32), pltpu.SemaphoreType.DMA((1,))],
        input_output_aliases={5: 0},
        compiler_params=pltpu.CompilerParams(vmem_limit_bytes=ROOM),
        cost_estimate=cost(2 * rows * width * E, 10 * MIB, MIB),
        name="outer",
    )(request_starts, decay_rate, returned, mid, act, inner)

    shared = swap(squares, "head")

    normed_output = pl.pallas_call(
        functools.partial(norm_kernel, float(width * groups)),
        out_shape=jax.ShapeDtypeStruct((rows, width), bf16),
        in_specs=[VMEM, VMEM, VMEM, VMEM],
        out_specs=HBM,
        scratch_shapes=[
            pltpu.VMEM((rows, width), bf16),
            pltpu.SemaphoreType.DMA((rows // E,)),
        ],
        compiler_params=pltpu.CompilerParams(vmem_limit_bytes=ROOM),
        cost_estimate=cost(6 * rows * width, 8 * MIB, rows * width),
        name="norm",
    )(shared, norm_gain.reshape(1, width), attended, gate_in)
    return (normed_output, final_states.reshape(1, heads, E, E))


def solution(mesh):
    placed = (
        P("ctx", "head"),
        P("ctx", "head"),
        P("ctx", "head"),
        P("ctx", "head"),
        P("head"),
        P("head"),
        P(),
        P(),
    )
    return jax.shard_map(
        per_device,
        mesh=mesh,
        in_specs=placed,
        out_specs=(P("ctx", "head"), P("ctx", "head", None, None)),
        check_vma=False,
    )
```

```python
import functools

import jax
import jax.numpy as jnp
from jax import lax
from jax.experimental import pallas as pl
from jax.experimental.pallas import tpu as pltpu
from jax.sharding import PartitionSpec as P

E = 128
ENDS_MOST = 2
SEGS = ENDS_MOST + 1
BLOCK = 512
TILE = 256
ABSENT = 1 << 20
FAR = 1e38
LOG2E = 1.4426950408889634
norm_eps = 1e-06
MIB = 1 << 20
LIMIT = 62 * MIB
ROOM = 40 * MIB
f32 = jnp.float32
bf16 = jnp.bfloat16
SMEM = pl.BlockSpec(memory_space=pltpu.SMEM)
VMEM = pl.BlockSpec(memory_space=pltpu.VMEM)
HBM = pl.BlockSpec(memory_space=pltpu.HBM)


def silu_wide(values):
    half = values.astype(f32) * 0.5
    return half + half * jnp.tanh(half)


def silu(values):
    return silu_wide(values).astype(bf16)


def rate_of(rates_ref, head):
    return jnp.maximum(rates_ref[head], 1e-30)


def end_of(starts_ref, request, stream):
    count = starts_ref.shape[0]
    following = starts_ref[jnp.minimum(request + 1, count - 1)]
    return jnp.where(request < count - 1, following - 1, stream - 1)


def local_ends(starts_ref, rows, ranks):
    stream = rows * ranks
    offset = lax.axis_index("ctx") * rows
    count = starts_ref.shape[0]
    first = jnp.int32(0)
    for request in range(count - 1):
        first += (starts_ref[request + 1] - 1 < offset).astype(jnp.int32)
    end_a = end_of(starts_ref, first, stream) - offset
    end_b = end_of(starts_ref, first + 1, stream) - offset
    end_b = jnp.where(first + 1 < count, end_b, ABSENT)
    return end_a, end_b


def power_of(rates_ref, head):
    return rate_of(rates_ref, head) * -LOG2E


def scalar_exp2(value):
    return jnp.exp2(jnp.full((1, E), value, f32))


def scalar_exp(value):
    return jnp.exp(jnp.full((1, E), value, f32))


def lanes(head):
    return pl.ds(pl.multiple_of(head * E, E), E)


def states_kernel(
    rows, ranks, starts_hbm, rates_hbm, k_hbm, v_hbm, sums_hbm, mid_hbm,
    starts_ref, rates_ref, k_raw, v_raw, gap, upto, sums, mids, sems, arrived, left,
):
    heads = k_raw.shape[1] // E
    small = (
        pltpu.make_async_copy(starts_hbm, starts_ref, sems.at[0]),
        pltpu.make_async_copy(rates_hbm, rates_ref, sems.at[1]),
    )

    def load(head):
        at = lanes(head)
        return (
            pltpu.make_async_copy(k_hbm.at[:, at], k_raw.at[:, at], arrived.at[0, head]),
            pltpu.make_async_copy(v_hbm.at[:, at], v_raw.at[:, at], arrived.at[1, head]),
        )

    share = sums.shape[0] // heads

    def store(head):
        pieces = pl.ds(head * share, share)
        return (
            pltpu.make_async_copy(sums.at[pieces], sums_hbm.at[pieces], left.at[0, head]),
            pltpu.make_async_copy(mids.at[head], mid_hbm.at[head], left.at[1, head]),
        )

    for copy in small:
        copy.start()
    for head in range(heads):
        for copy in load(head):
            copy.start()
    for copy in small:
        copy.wait()
    end_a, end_b = local_ends(starts_ref, rows, ranks)
    token = lax.broadcasted_iota(jnp.int32, (rows, E), 0)
    in_a = token <= end_a
    in_b = token <= end_b
    place = lax.broadcasted_iota(jnp.int32, (8, rows), 1)
    place_end = jnp.where(place <= end_a, end_a, jnp.where(place <= end_b, end_b, ABSENT))
    last = (place // BLOCK) * BLOCK + (BLOCK - 1)
    gap[...] = (jnp.minimum(place_end, last) - place).astype(f32)
    upto[0] = jnp.where(in_a, 1.0, 0.0)
    upto[1] = jnp.where(in_b, 1.0, 0.0)
    at_mid = (end_a < BLOCK - 1).astype(jnp.int32) + (end_b < BLOCK - 1).astype(jnp.int32)

    def work(head):
        at = lanes(head)
        power = power_of(rates_ref, head)
        parts = []
        for first in range(0, rows, BLOCK):
            span = pl.ds(first, BLOCK)
            keys = silu(k_raw[span, at].T)
            values = silu_wide(v_raw[span, at])
            decay = jnp.exp2(gap[:, span] * power)
            scaled = (keys.astype(f32) * decay[:1, :]).astype(bf16)
            spread = jnp.concatenate(
                [
                    (values * upto[0, span, :]).astype(bf16),
                    (values * upto[1, span, :]).astype(bf16),
                    values.astype(bf16),
                ],
                axis=1,
            )
            running = jnp.dot(scaled, spread, preferred_element_type=f32)
            until_a, until_b, until_c = (running[:, x * E : (x + 1) * E] for x in range(SEGS))
            parts.append((until_a, until_b - until_a, until_c - until_b))
        early, late = parts
        mid = jnp.zeros((E, E), f32)
        for x, end in enumerate((end_a, end_b, jnp.int32(ABSENT))):
            reach = jnp.maximum(jnp.minimum(end, rows - 1) - (BLOCK - 1), 0).astype(f32)
            total = early[x] * scalar_exp2(reach * power) + late[x]
            sums[pl.ds(head * share, share), x] = total.astype(bf16).reshape(share, -1, E)
            mid += early[x] * (at_mid == x).astype(f32)
        mids[head] = mid

    @pl.loop(0, heads // 2)
    def _(group):
        mine = [group * 2 + index for index in range(2)]
        for head in mine:
            for copy in load(head):
                copy.wait()
        for head in mine:
            work(head)
        for head in mine:
            for copy in store(head):
                copy.start()

    for head in range(heads):
        for copy in store(head):
            copy.wait()


def request_ends(starts_ref, rows, ranks):
    count = starts_ref.shape[0]
    ends = [
        starts_ref[r + 1] - 1 if r + 1 < count else jnp.int32(rows * ranks - 1)
        for r in range(count)
    ]
    return ends, [end // rows for end in ends]


def advance(rows, rate, homes, got_ref, counts, keep):
    ranks = got_ref.shape[0]
    for p in range(ranks):
        counts[p] = 0
    for home in homes:
        counts[home] = counts[home] + 1
    whole = scalar_exp(float(rows) * -rate)
    state = jnp.zeros(got_ref.shape[2:], f32)
    for p in range(ranks):
        keep(p, state)
        ended = counts[p]
        state = got_ref[p, ended].astype(f32) + state * (whole * (ended == 0).astype(f32))


def my_rate(rates_ref, ranks):
    return rate_of(rates_ref, lax.axis_index("ctx") * rates_ref.shape[0] // ranks)


def scan_kernel(
    rows, starts_ref, slots_ref, rates_ref, got_ref, inner_hbm, back_ref, counts, carried
):
    ranks = got_ref.shape[0]
    rate = my_rate(rates_ref, ranks)
    ends, homes = request_ends(starts_ref, rows, ranks)

    def keep(p, state):
        carried[p] = state
        back_ref[p, 0] = state.astype(bf16)

    advance(rows, rate, homes, got_ref, counts, keep)
    for r, (end, home) in enumerate(zip(ends, homes)):
        second = home == homes[r - 1] if r else jnp.bool_(False)
        lead = scalar_exp((end - home * rows + 1).astype(f32) * -rate)
        lead = lead * jnp.where(second, 0.0, 1.0)
        final = got_ref[home, second.astype(jnp.int32)].astype(f32) + carried[home] * lead
        back_ref[slots_ref[r], 1] = final.astype(bf16)


def inner_kernel(
    rows, ranks, starts_ref, rates_ref, q_hbm, k_hbm, v_hbm, inner_hbm, act_hbm,
    q_raw, k_raw, v_raw, inner, act, dist, arrived, left,
):
    heads = q_raw.shape[1] // E

    def load(head):
        at = lanes(head)
        return (
            pltpu.make_async_copy(q_hbm.at[:, at], q_raw.at[:, at], arrived.at[0, head]),
            pltpu.make_async_copy(k_hbm.at[:, at], k_raw.at[:, at], arrived.at[1, head]),
            pltpu.make_async_copy(v_hbm.at[:, at], v_raw.at[:, at], arrived.at[2, head]),
        )

    def store(head):
        at = lanes(head)
        return (
            pltpu.make_async_copy(inner.at[:, at], inner_hbm.at[:, at], left.at[0, head]),
            pltpu.make_async_copy(act.at[:, at], act_hbm.at[:, at], left.at[1, head]),
        )

    for head in range(heads):
        for copy in load(head):
            copy.start()
    end_a, end_b = local_ends(starts_ref, rows, ranks)
    for block in range(rows // BLOCK):
        t = lax.broadcasted_iota(jnp.int32, (BLOCK, BLOCK), 0)
        s = lax.broadcasted_iota(jnp.int32, (BLOCK, BLOCK), 1)
        here = t + block * BLOCK
        begin = jnp.where(here <= end_a, 0, jnp.where(here <= end_b, end_a + 1, end_b + 1))
        keep = (s <= t) & (s + block * BLOCK >= begin)
        dist[block] = jnp.where(keep, (t - s).astype(f32), FAR)

    @pl.loop(0, heads)
    def _(head):
        at = lanes(head)
        power = power_of(rates_ref, head)
        for copy in load(head):
            copy.wait()
        act[:, at] = silu(q_raw[:, at])
        keys = silu(k_raw[:, at])
        values = silu(v_raw[:, at])
        for block in range(rows // BLOCK):
            base = block * BLOCK
            for top in range(0, BLOCK, TILE):
                wide = top + TILE
                mine = pl.ds(base + top, TILE)
                scores = lax.dot_general(
                    act[mine, at],
                    keys[base : base + wide],
                    (((1,), (1,)), ((), ())),
                    preferred_element_type=f32,
                )
                decay = jnp.exp2(dist[block, top : top + TILE, :wide] * power)
                weights = (scores * decay).astype(bf16)
                inner[mine, at] = jnp.dot(
                    weights, values[base : base + wide], preferred_element_type=f32
                )
        for copy in store(head):
            copy.start()

    for head in range(heads):
        for copy in store(head):
            copy.wait()


def outer_kernel(
    rows, ranks, starts_ref, rates_ref, back_ref, mid_ref, act_ref, inner_ref,
    out_ref, final_hbm, squares_ref, total, lead, left,
):
    heads = mid_ref.shape[0]
    share = back_ref.shape[0] // heads
    finals = pltpu.make_async_copy(back_ref.at[:, 1], final_hbm, left.at[0])
    finals.start()
    end_a, end_b = local_ends(starts_ref, rows, ranks)
    mid_end = jnp.where(end_a >= BLOCK - 1, end_a, jnp.where(end_b >= BLOCK - 1, end_b, ABSENT))
    from_before = (end_a >= BLOCK - 1).astype(f32)
    total[...] = jnp.zeros_like(total)
    steps = lax.broadcasted_iota(jnp.int32, (BLOCK, E), 0)
    for block, last in enumerate((end_a, mid_end)):
        here = steps + block * BLOCK <= last
        lead[block] = jnp.where(here, (steps + 1).astype(f32), FAR)

    @pl.loop(0, heads, unroll=4)
    def _(head):
        at = lanes(head)
        power = power_of(rates_ref, head)
        incoming = back_ref[pl.ds(head * share, share), 0].reshape(E, E)
        later = mid_ref[head] + incoming.astype(f32) * (
            scalar_exp2(float(BLOCK) * power) * from_before
        )
        for block, state in enumerate((incoming, later.astype(bf16))):
            span = pl.ds(block * BLOCK, BLOCK)
            outer = jnp.dot(act_ref[span, at], state, preferred_element_type=f32)
            attended = inner_ref[span, at] + outer * jnp.exp2(lead[block] * power)
            out_ref[span, at] = attended
            total[span, :] += attended * attended

    row_sums = jnp.concatenate(
        [
            jnp.sum(total[first : first + E, :].T, axis=0, keepdims=True)
            for first in range(0, rows, E)
        ],
        axis=0,
    )
    squares_ref[...] = jnp.broadcast_to(row_sums[None], squares_ref.shape)
    finals.wait()


def norm_kernel(
    features, squares_ref, gain_ref, att_ref, gate_ref, out_hbm, out, sems
):
    bands = out.shape[0] // E

    def store(band):
        span = pl.ds(band * E, E)
        return pltpu.make_async_copy(out.at[span, :], out_hbm.at[span, :], sems.at[band])

    total = jnp.sum(squares_ref[...], axis=0)
    scale = 0.5 * lax.rsqrt(total * (1.0 / features) + norm_eps)
    for band in range(bands):
        span = pl.ds(band * E, E)
        column = jnp.broadcast_to(scale[band : band + 1], (E, E)).T
        for first in range(0, out.shape[1], E):
            cols = slice(first, first + E)
            opened = 1.0 + jnp.tanh(0.5 * gate_ref[span, cols].astype(f32))
            scaled = att_ref[span, cols] * column * gain_ref[:, cols]
            out[span, cols] = (scaled * opened).astype(bf16)
        store(band).start()
    for band in range(bands):
        store(band).wait()


def cost(flops, moved, hard):
    return pl.CostEstimate(flops=int(flops), bytes_accessed=int(moved), transcendentals=int(hard))


def swap(array, axis):
    return lax.all_to_all(array, axis, split_axis=0, concat_axis=0, tiled=True)


def per_device(
    query, key_in, value_in, gate_in, norm_gain, decay_rate, request_starts, request_slots
):
    return local(
        lax.axis_size("ctx"), lax.axis_size("head"), query, key_in, value_in, gate_in, norm_gain,
        decay_rate, request_starts, request_slots,
    )


def local(
    ranks, groups, query, key_in, value_in, gate_in, norm_gain, decay_rate, request_starts,
    request_slots,
):
    rows, width = query.shape
    heads = decay_rate.shape[0]
    piece = E * heads // ranks

    sums, mid = pl.pallas_call(
        functools.partial(states_kernel, rows, ranks),
        out_shape=(
            jax.ShapeDtypeStruct((ranks, SEGS, piece, E), bf16),
            jax.ShapeDtypeStruct((heads, E, E), f32),
        ),
        in_specs=[HBM, HBM, HBM, HBM],
        out_specs=(HBM, HBM),
        scratch_shapes=[
            pltpu.SMEM(request_starts.shape, jnp.int32),
            pltpu.SMEM(decay_rate.shape, f32),
            pltpu.VMEM((rows, width), bf16),
            pltpu.VMEM((rows, width), bf16),
            pltpu.VMEM((8, rows), f32),
            pltpu.VMEM((ENDS_MOST, rows, E), f32),
            pltpu.VMEM((ranks, SEGS, piece, E), bf16),
            pltpu.VMEM((heads, E, E), f32),
            pltpu.SemaphoreType.DMA((2,)),
            pltpu.SemaphoreType.DMA((2, heads)),
            pltpu.SemaphoreType.DMA((2, heads)),
        ],
        compiler_params=pltpu.CompilerParams(vmem_limit_bytes=LIMIT),
        cost_estimate=cost(2 * rows * width * E * SEGS, 5 * MIB, 3 * rows * width),
        name="states",
    )(request_starts, decay_rate, key_in, value_in)

    got = swap(sums, "ctx")

    inner, act = pl.pallas_call(
        functools.partial(inner_kernel, rows, ranks),
        out_shape=(
            jax.ShapeDtypeStruct((rows, width), f32),
            jax.ShapeDtypeStruct((rows, width), bf16),
        ),
        in_specs=[SMEM, SMEM, HBM, HBM, HBM],
        out_specs=(HBM, HBM),
        scratch_shapes=[
            pltpu.VMEM((rows, width), bf16),
            pltpu.VMEM((rows, width), bf16),
            pltpu.VMEM((rows, width), bf16),
            pltpu.VMEM((rows, width), f32),
            pltpu.VMEM((rows, width), bf16),
            pltpu.VMEM((rows // BLOCK, BLOCK, BLOCK), f32),
            pltpu.SemaphoreType.DMA((3, heads)),
            pltpu.SemaphoreType.DMA((2, heads)),
        ],
        compiler_params=pltpu.CompilerParams(vmem_limit_bytes=LIMIT),
        cost_estimate=cost(4 * rows * width * BLOCK, 12 * rows * width, rows * width * 8),
        name="inner",
    )(request_starts, decay_rate, query, key_in, value_in)

    back = pl.pallas_call(
        functools.partial(scan_kernel, rows),
        out_shape=jax.ShapeDtypeStruct((ranks, 2, piece, E), bf16),
        in_specs=[SMEM, SMEM, SMEM, VMEM, HBM],
        out_specs=VMEM,
        scratch_shapes=[pltpu.SMEM((ranks,), jnp.int32), pltpu.VMEM((ranks, piece, E), f32)],
        compiler_params=pltpu.CompilerParams(vmem_limit_bytes=50 * MIB),
        cost_estimate=cost(MIB, 2 * MIB, 0),
        name="scan",
    )(request_starts, request_slots, decay_rate, got, inner)

    returned = swap(back, "ctx")

    attended, final_states, squares = pl.pallas_call(
        functools.partial(outer_kernel, rows, ranks),
        out_shape=(
            jax.ShapeDtypeStruct((rows, width), f32),
            jax.ShapeDtypeStruct((ranks, piece, E), bf16),
            jax.ShapeDtypeStruct((groups, rows // E, E), f32),
        ),
        in_specs=[SMEM, SMEM, VMEM, VMEM, VMEM, VMEM],
        out_specs=(VMEM, HBM, VMEM),
        scratch_shapes=[
            pltpu.VMEM((rows, E), f32),
            pltpu.VMEM((rows // BLOCK, BLOCK, E), f32),
            pltpu.SemaphoreType.DMA((1,)),
        ],
        input_output_aliases={5: 0},
        compiler_params=pltpu.CompilerParams(vmem_limit_bytes=ROOM),
        cost_estimate=cost(2 * rows * width * E, 10 * MIB, MIB),
        name="outer",
    )(request_starts, decay_rate, returned, mid, act, inner)

    shared = swap(squares, "head")

    normed_output = pl.pallas_call(
        functools.partial(norm_kernel, float(width * groups)),
        out_shape=jax.ShapeDtypeStruct((rows, width), bf16),
        in_specs=[VMEM, VMEM, VMEM, VMEM],
        out_specs=HBM,
        scratch_shapes=[
            pltpu.VMEM((rows, width), bf16),
            pltpu.SemaphoreType.DMA((rows // E,)),
        ],
        compiler_params=pltpu.CompilerParams(vmem_limit_bytes=ROOM),
        cost_estimate=cost(6 * rows * width, 8 * MIB, rows * width),
        name="norm",
    )(shared, norm_gain.reshape(1, width), attended, gate_in)
    return (normed_output, final_states.reshape(1, heads, E, E))


def solution(mesh):
    placed = (
        P("ctx", "head"),
        P("ctx", "head"),
        P("ctx", "head"),
        P("ctx", "head"),
        P("head"),
        P("head"),
        P(),
        P(),
    )
    return jax.shard_map(
        per_device,
        mesh=mesh,
        in_specs=placed,
        out_specs=(P("ctx", "head"), P("ctx", "head", None, None)),
        check_vma=False,
    )
```

```python
import functools

import jax
import jax.numpy as jnp
from jax import lax
from jax.experimental import pallas as pl
from jax.experimental.pallas import tpu as pltpu
from jax.sharding import PartitionSpec as P

E = 128
ENDS_MOST = 2
SEGS = ENDS_MOST + 1
BLOCK = 512
TILE = 256
ABSENT = 1 << 20
FAR = 1e38
LOG2E = 1.4426950408889634
norm_eps = 1e-06
MIB = 1 << 20
LIMIT = 62 * MIB
ROOM = 40 * MIB
f32 = jnp.float32
bf16 = jnp.bfloat16
SMEM = pl.BlockSpec(memory_space=pltpu.SMEM)
VMEM = pl.BlockSpec(memory_space=pltpu.VMEM)
HBM = pl.BlockSpec(memory_space=pltpu.HBM)


def silu_wide(values):
    half = values.astype(f32) * 0.5
    return half + half * jnp.tanh(half)


def silu(values):
    return silu_wide(values).astype(bf16)


def rate_of(rates_ref, head):
    return jnp.maximum(rates_ref[head], 1e-30)


def end_of(starts_ref, request, stream):
    count = starts_ref.shape[0]
    following = starts_ref[jnp.minimum(request + 1, count - 1)]
    return jnp.where(request < count - 1, following - 1, stream - 1)


def local_ends(starts_ref, rows, ranks):
    stream = rows * ranks
    offset = lax.axis_index("ctx") * rows
    count = starts_ref.shape[0]
    first = jnp.int32(0)
    for request in range(count - 1):
        first += (starts_ref[request + 1] - 1 < offset).astype(jnp.int32)
    end_a = end_of(starts_ref, first, stream) - offset
    end_b = end_of(starts_ref, first + 1, stream) - offset
    end_b = jnp.where(first + 1 < count, end_b, ABSENT)
    return end_a, end_b


def power_of(rates_ref, head):
    return rate_of(rates_ref, head) * -LOG2E


def scalar_exp2(value):
    return jnp.exp2(jnp.full((1, E), value, f32))


def scalar_exp(value):
    return jnp.exp(jnp.full((1, E), value, f32))


def lanes(head):
    return pl.ds(pl.multiple_of(head * E, E), E)


def states_kernel(
    rows, ranks, starts_hbm, rates_hbm, k_hbm, v_hbm, sums_hbm, mid_hbm,
    starts_ref, rates_ref, k_raw, v_raw, gap, upto, sums, mids, sems, arrived, left,
):
    heads = k_raw.shape[1] // E
    small = (
        pltpu.make_async_copy(starts_hbm, starts_ref, sems.at[0]),
        pltpu.make_async_copy(rates_hbm, rates_ref, sems.at[1]),
    )

    def load(head):
        at = lanes(head)
        return (
            pltpu.make_async_copy(k_hbm.at[:, at], k_raw.at[:, at], arrived.at[0, head]),
            pltpu.make_async_copy(v_hbm.at[:, at], v_raw.at[:, at], arrived.at[1, head]),
        )

    share = sums.shape[0] // heads

    def store(head):
        pieces = pl.ds(head * share, share)
        return (
            pltpu.make_async_copy(sums.at[pieces], sums_hbm.at[pieces], left.at[0, head]),
            pltpu.make_async_copy(mids.at[head], mid_hbm.at[head], left.at[1, head]),
        )

    for copy in small:
        copy.start()
    for head in range(heads):
        for copy in load(head):
            copy.start()
    for copy in small:
        copy.wait()
    end_a, end_b = local_ends(starts_ref, rows, ranks)
    token = lax.broadcasted_iota(jnp.int32, (rows, E), 0)
    in_a = token <= end_a
    in_b = token <= end_b
    place = lax.broadcasted_iota(jnp.int32, (8, rows), 1)
    place_end = jnp.where(place <= end_a, end_a, jnp.where(place <= end_b, end_b, ABSENT))
    last = (place // BLOCK) * BLOCK + (BLOCK - 1)
    gap[...] = (jnp.minimum(place_end, last) - place).astype(f32)
    upto[0] = jnp.where(in_a, 1.0, 0.0)
    upto[1] = jnp.where(in_b, 1.0, 0.0)
    at_mid = (end_a < BLOCK - 1).astype(jnp.int32) + (end_b < BLOCK - 1).astype(jnp.int32)

    def work(head):
        at = lanes(head)
        power = power_of(rates_ref, head)
        parts = []
        for first in range(0, rows, BLOCK):
            span = pl.ds(first, BLOCK)
            keys = silu(k_raw[span, at].T)
            values = silu_wide(v_raw[span, at])
            decay = jnp.exp2(gap[:, span] * power)
            scaled = (keys.astype(f32) * decay[:1, :]).astype(bf16)
            spread = jnp.concatenate(
                [
                    (values * upto[0, span, :]).astype(bf16),
                    (values * upto[1, span, :]).astype(bf16),
                    values.astype(bf16),
                ],
                axis=1,
            )
            running = jnp.dot(scaled, spread, preferred_element_type=f32)
            until_a, until_b, until_c = (running[:, x * E : (x + 1) * E] for x in range(SEGS))
            parts.append((until_a, until_b - until_a, until_c - until_b))
        early, late = parts
        mid = jnp.zeros((E, E), f32)
        for x, end in enumerate((end_a, end_b, jnp.int32(ABSENT))):
            reach = jnp.maximum(jnp.minimum(end, rows - 1) - (BLOCK - 1), 0).astype(f32)
            total = early[x] * scalar_exp2(reach * power) + late[x]
            sums[pl.ds(head * share, share), x] = total.astype(bf16).reshape(share, -1, E)
            mid += early[x] * (at_mid == x).astype(f32)
        mids[head] = mid

    @pl.loop(0, heads // 2)
    def _(group):
        mine = [group * 2 + index for index in range(2)]
        for head in mine:
            for copy in load(head):
                copy.wait()
        for head in mine:
            work(head)
        for head in mine:
            for copy in store(head):
                copy.start()

    for head in range(heads):
        for copy in store(head):
            copy.wait()


def request_ends(starts_ref, rows, ranks):
    count = starts_ref.shape[0]
    ends = [
        starts_ref[r + 1] - 1 if r + 1 < count else jnp.int32(rows * ranks - 1)
        for r in range(count)
    ]
    return ends, [end // rows for end in ends]


def advance(rows, rate, homes, got_ref, counts, keep):
    ranks = got_ref.shape[0]
    for p in range(ranks):
        counts[p] = 0
    for home in homes:
        counts[home] = counts[home] + 1
    whole = scalar_exp(float(rows) * -rate)
    state = jnp.zeros(got_ref.shape[2:], f32)
    for p in range(ranks):
        keep(p, state)
        ended = counts[p]
        state = got_ref[p, ended].astype(f32) + state * (whole * (ended == 0).astype(f32))


def my_rate(rates_ref, ranks):
    return rate_of(rates_ref, lax.axis_index("ctx") * rates_ref.shape[0] // ranks)


def scan_kernel(
    rows, starts_ref, slots_ref, rates_ref, got_ref, inner_hbm, back_ref, counts, carried
):
    ranks = got_ref.shape[0]
    rate = my_rate(rates_ref, ranks)
    ends, homes = request_ends(starts_ref, rows, ranks)

    def keep(p, state):
        carried[p] = state
        back_ref[p, 0] = state.astype(bf16)

    advance(rows, rate, homes, got_ref, counts, keep)
    for r, (end, home) in enumerate(zip(ends, homes)):
        second = home == homes[r - 1] if r else jnp.bool_(False)
        lead = scalar_exp((end - home * rows + 1).astype(f32) * -rate)
        lead = lead * jnp.where(second, 0.0, 1.0)
        final = got_ref[home, second.astype(jnp.int32)].astype(f32) + carried[home] * lead
        back_ref[slots_ref[r], 1] = final.astype(bf16)


def inner_kernel(
    rows, ranks, starts_ref, rates_ref, gain_ref, q_hbm, k_hbm, v_hbm, gate_hbm,
    inner_hbm, act_hbm, gated_hbm,
    q_raw, k_raw, v_raw, gate_raw, inner, act, gated, dist, arrived, left,
):
    heads = q_raw.shape[1] // E

    def load(head):
        at = lanes(head)
        return (
            pltpu.make_async_copy(q_hbm.at[:, at], q_raw.at[:, at], arrived.at[0, head]),
            pltpu.make_async_copy(k_hbm.at[:, at], k_raw.at[:, at], arrived.at[1, head]),
            pltpu.make_async_copy(v_hbm.at[:, at], v_raw.at[:, at], arrived.at[2, head]),
            pltpu.make_async_copy(gate_hbm.at[:, at], gate_raw.at[:, at], arrived.at[3, head]),
        )

    def store(head):
        at = lanes(head)
        return (
            pltpu.make_async_copy(inner.at[:, at], inner_hbm.at[:, at], left.at[0, head]),
            pltpu.make_async_copy(act.at[:, at], act_hbm.at[:, at], left.at[1, head]),
            pltpu.make_async_copy(gated.at[:, at], gated_hbm.at[:, at], left.at[2, head]),
        )

    for head in range(heads):
        for copy in load(head):
            copy.start()
    end_a, end_b = local_ends(starts_ref, rows, ranks)
    for block in range(rows // BLOCK):
        t = lax.broadcasted_iota(jnp.int32, (BLOCK, BLOCK), 0)
        s = lax.broadcasted_iota(jnp.int32, (BLOCK, BLOCK), 1)
        here = t + block * BLOCK
        begin = jnp.where(here <= end_a, 0, jnp.where(here <= end_b, end_a + 1, end_b + 1))
        keep = (s <= t) & (s + block * BLOCK >= begin)
        dist[block] = jnp.where(keep, (t - s).astype(f32), FAR)

    @pl.loop(0, heads)
    def _(head):
        at = lanes(head)
        power = power_of(rates_ref, head)
        for copy in load(head):
            copy.wait()
        act[:, at] = silu(q_raw[:, at])
        opened = 1.0 + jnp.tanh(0.5 * gate_raw[:, at].astype(f32))
        gated[:, at] = opened * (0.5 * gain_ref[:, at])
        keys = silu(k_raw[:, at])
        values = silu(v_raw[:, at])
        for block in range(rows // BLOCK):
            base = block * BLOCK
            for top in range(0, BLOCK, TILE):
                wide = top + TILE
                mine = pl.ds(base + top, TILE)
                scores = lax.dot_general(
                    act[mine, at],
                    keys[base : base + wide],
                    (((1,), (1,)), ((), ())),
                    preferred_element_type=f32,
                )
                decay = jnp.exp2(dist[block, top : top + TILE, :wide] * power)
                weights = (scores * decay).astype(bf16)
                inner[mine, at] = jnp.dot(
                    weights, values[base : base + wide], preferred_element_type=f32
                )
        for copy in store(head):
            copy.start()

    for head in range(heads):
        for copy in store(head):
            copy.wait()


def outer_kernel(
    rows, ranks, starts_ref, rates_ref, back_ref, mid_ref, act_ref, inner_ref,
    out_ref, final_hbm, squares_ref, total, lead, left,
):
    heads = mid_ref.shape[0]
    share = back_ref.shape[0] // heads
    finals = pltpu.make_async_copy(back_ref.at[:, 1], final_hbm, left.at[0])
    finals.start()
    end_a, end_b = local_ends(starts_ref, rows, ranks)
    mid_end = jnp.where(end_a >= BLOCK - 1, end_a, jnp.where(end_b >= BLOCK - 1, end_b, ABSENT))
    from_before = (end_a >= BLOCK - 1).astype(f32)
    total[...] = jnp.zeros_like(total)
    steps = lax.broadcasted_iota(jnp.int32, (BLOCK, E), 0)
    for block, last in enumerate((end_a, mid_end)):
        here = steps + block * BLOCK <= last
        lead[block] = jnp.where(here, (steps + 1).astype(f32), FAR)

    @pl.loop(0, heads, unroll=4)
    def _(head):
        at = lanes(head)
        power = power_of(rates_ref, head)
        incoming = back_ref[pl.ds(head * share, share), 0].reshape(E, E)
        later = mid_ref[head] + incoming.astype(f32) * (
            scalar_exp2(float(BLOCK) * power) * from_before
        )
        for block, state in enumerate((incoming, later.astype(bf16))):
            span = pl.ds(block * BLOCK, BLOCK)
            outer = jnp.dot(act_ref[span, at], state, preferred_element_type=f32)
            attended = inner_ref[span, at] + outer * jnp.exp2(lead[block] * power)
            out_ref[span, at] = attended
            total[span, :] += attended * attended

    row_sums = jnp.concatenate(
        [
            jnp.sum(total[first : first + E, :].T, axis=0, keepdims=True)
            for first in range(0, rows, E)
        ],
        axis=0,
    )
    squares_ref[...] = jnp.broadcast_to(row_sums[None], squares_ref.shape)
    finals.wait()


def norm_kernel(
    features, squares_ref, att_ref, gated_ref, out_hbm, out, sems
):
    bands = out.shape[0] // E

    def store(band):
        span = pl.ds(band * E, E)
        return pltpu.make_async_copy(out.at[span, :], out_hbm.at[span, :], sems.at[band])

    total = jnp.sum(squares_ref[...], axis=0)
    scale = lax.rsqrt(total * (1.0 / features) + norm_eps)
    for band in range(bands):
        span = pl.ds(band * E, E)
        column = jnp.broadcast_to(scale[band : band + 1], (E, E)).T
        for first in range(0, out.shape[1], E):
            cols = slice(first, first + E)
            out[span, cols] = (att_ref[span, cols] * column * gated_ref[span, cols]).astype(bf16)
        store(band).start()
    for band in range(bands):
        store(band).wait()


def cost(flops, moved, hard):
    return pl.CostEstimate(flops=int(flops), bytes_accessed=int(moved), transcendentals=int(hard))


def swap(array, axis):
    return lax.all_to_all(array, axis, split_axis=0, concat_axis=0, tiled=True)


def per_device(
    query, key_in, value_in, gate_in, norm_gain, decay_rate, request_starts, request_slots
):
    return local(
        lax.axis_size("ctx"), lax.axis_size("head"), query, key_in, value_in, gate_in, norm_gain,
        decay_rate, request_starts, request_slots,
    )


def local(
    ranks, groups, query, key_in, value_in, gate_in, norm_gain, decay_rate, request_starts,
    request_slots,
):
    rows, width = query.shape
    heads = decay_rate.shape[0]
    piece = E * heads // ranks

    sums, mid = pl.pallas_call(
        functools.partial(states_kernel, rows, ranks),
        out_shape=(
            jax.ShapeDtypeStruct((ranks, SEGS, piece, E), bf16),
            jax.ShapeDtypeStruct((heads, E, E), f32),
        ),
        in_specs=[HBM, HBM, HBM, HBM],
        out_specs=(HBM, HBM),
        scratch_shapes=[
            pltpu.SMEM(request_starts.shape, jnp.int32),
            pltpu.SMEM(decay_rate.shape, f32),
            pltpu.VMEM((rows, width), bf16),
            pltpu.VMEM((rows, width), bf16),
            pltpu.VMEM((8, rows), f32),
            pltpu.VMEM((ENDS_MOST, rows, E), f32),
            pltpu.VMEM((ranks, SEGS, piece, E), bf16),
            pltpu.VMEM((heads, E, E), f32),
            pltpu.SemaphoreType.DMA((2,)),
            pltpu.SemaphoreType.DMA((2, heads)),
            pltpu.SemaphoreType.DMA((2, heads)),
        ],
        compiler_params=pltpu.CompilerParams(vmem_limit_bytes=LIMIT),
        cost_estimate=cost(2 * rows * width * E * SEGS, 5 * MIB, 3 * rows * width),
        name="states",
    )(request_starts, decay_rate, key_in, value_in)

    got = swap(sums, "ctx")

    inner, act, gated = pl.pallas_call(
        functools.partial(inner_kernel, rows, ranks),
        out_shape=(
            jax.ShapeDtypeStruct((rows, width), f32),
            jax.ShapeDtypeStruct((rows, width), bf16),
            jax.ShapeDtypeStruct((rows, width), f32),
        ),
        in_specs=[SMEM, SMEM, VMEM, HBM, HBM, HBM, HBM],
        out_specs=(HBM, HBM, HBM),
        scratch_shapes=[
            pltpu.VMEM((rows, width), bf16),
            pltpu.VMEM((rows, width), bf16),
            pltpu.VMEM((rows, width), bf16),
            pltpu.VMEM((rows, width), bf16),
            pltpu.VMEM((rows, width), f32),
            pltpu.VMEM((rows, width), bf16),
            pltpu.VMEM((rows, width), f32),
            pltpu.VMEM((rows // BLOCK, BLOCK, BLOCK), f32),
            pltpu.SemaphoreType.DMA((4, heads)),
            pltpu.SemaphoreType.DMA((3, heads)),
        ],
        compiler_params=pltpu.CompilerParams(vmem_limit_bytes=LIMIT),
        cost_estimate=cost(4 * rows * width * BLOCK, 12 * rows * width, rows * width * 8),
        name="inner",
    )(request_starts, decay_rate, norm_gain.reshape(1, width), query, key_in, value_in, gate_in)

    back = pl.pallas_call(
        functools.partial(scan_kernel, rows),
        out_shape=jax.ShapeDtypeStruct((ranks, 2, piece, E), bf16),
        in_specs=[SMEM, SMEM, SMEM, VMEM, HBM],
        out_specs=VMEM,
        scratch_shapes=[pltpu.SMEM((ranks,), jnp.int32), pltpu.VMEM((ranks, piece, E), f32)],
        compiler_params=pltpu.CompilerParams(vmem_limit_bytes=50 * MIB),
        cost_estimate=cost(MIB, 2 * MIB, 0),
        name="scan",
    )(request_starts, request_slots, decay_rate, got, inner)

    returned = swap(back, "ctx")

    attended, final_states, squares = pl.pallas_call(
        functools.partial(outer_kernel, rows, ranks),
        out_shape=(
            jax.ShapeDtypeStruct((rows, width), f32),
            jax.ShapeDtypeStruct((ranks, piece, E), bf16),
            jax.ShapeDtypeStruct((groups, rows // E, E), f32),
        ),
        in_specs=[SMEM, SMEM, VMEM, VMEM, VMEM, VMEM],
        out_specs=(VMEM, HBM, VMEM),
        scratch_shapes=[
            pltpu.VMEM((rows, E), f32),
            pltpu.VMEM((rows // BLOCK, BLOCK, E), f32),
            pltpu.SemaphoreType.DMA((1,)),
        ],
        input_output_aliases={5: 0},
        compiler_params=pltpu.CompilerParams(vmem_limit_bytes=ROOM),
        cost_estimate=cost(2 * rows * width * E, 10 * MIB, MIB),
        name="outer",
    )(request_starts, decay_rate, returned, mid, act, inner)

    shared = swap(squares, "head")

    normed_output = pl.pallas_call(
        functools.partial(norm_kernel, float(width * groups)),
        out_shape=jax.ShapeDtypeStruct((rows, width), bf16),
        in_specs=[VMEM, VMEM, VMEM],
        out_specs=HBM,
        scratch_shapes=[
            pltpu.VMEM((rows, width), bf16),
            pltpu.SemaphoreType.DMA((rows // E,)),
        ],
        compiler_params=pltpu.CompilerParams(vmem_limit_bytes=ROOM),
        cost_estimate=cost(6 * rows * width, 8 * MIB, rows * width),
        name="norm",
    )(shared, attended, gated)
    return (normed_output, final_states.reshape(1, heads, E, E))


def solution(mesh):
    placed = (
        P("ctx", "head"),
        P("ctx", "head"),
        P("ctx", "head"),
        P("ctx", "head"),
        P("head"),
        P("head"),
        P(),
        P(),
    )
    return jax.shard_map(
        per_device,
        mesh=mesh,
        in_specs=placed,
        out_specs=(P("ctx", "head"), P("ctx", "head", None, None)),
        check_vma=False,
    )
```

```python
import functools

import jax
import jax.numpy as jnp
from jax import lax
from jax.experimental import pallas as pl
from jax.experimental.pallas import tpu as pltpu
from jax.sharding import PartitionSpec as P

E = 128
ENDS_MOST = 2
SEGS = ENDS_MOST + 1
BLOCK = 512
TILE = 256
ABSENT = 1 << 20
FAR = 1e38
LOG2E = 1.4426950408889634
norm_eps = 1e-06
MIB = 1 << 20
LIMIT = 62 * MIB
ROOM = 40 * MIB
f32 = jnp.float32
bf16 = jnp.bfloat16
SMEM = pl.BlockSpec(memory_space=pltpu.SMEM)
VMEM = pl.BlockSpec(memory_space=pltpu.VMEM)
HBM = pl.BlockSpec(memory_space=pltpu.HBM)


def silu_wide(values):
    half = values.astype(f32) * 0.5
    return half + half * jnp.tanh(half)


def silu(values):
    return silu_wide(values).astype(bf16)


def rate_of(rates_ref, head):
    return jnp.maximum(rates_ref[head], 1e-30)


def end_of(starts_ref, request, stream):
    count = starts_ref.shape[0]
    following = starts_ref[jnp.minimum(request + 1, count - 1)]
    return jnp.where(request < count - 1, following - 1, stream - 1)


def local_ends(starts_ref, rows, ranks):
    stream = rows * ranks
    offset = lax.axis_index("ctx") * rows
    count = starts_ref.shape[0]
    first = jnp.int32(0)
    for request in range(count - 1):
        first += (starts_ref[request + 1] - 1 < offset).astype(jnp.int32)
    end_a = end_of(starts_ref, first, stream) - offset
    end_b = end_of(starts_ref, first + 1, stream) - offset
    end_b = jnp.where(first + 1 < count, end_b, ABSENT)
    return end_a, end_b


def power_of(rates_ref, head):
    return rate_of(rates_ref, head) * -LOG2E


def scalar_exp2(value):
    return jnp.exp2(jnp.full((1, E), value, f32))


def scalar_exp(value):
    return jnp.exp(jnp.full((1, E), value, f32))


def lanes(head):
    return pl.ds(pl.multiple_of(head * E, E), E)


def states_kernel(
    rows, ranks, starts_hbm, rates_hbm, k_hbm, v_hbm, sums_hbm,
    starts_ref, rates_ref, k_raw, v_raw, gap, upto, sums, sems, arrived, left,
):
    heads = k_raw.shape[1] // E
    small = (
        pltpu.make_async_copy(starts_hbm, starts_ref, sems.at[0]),
        pltpu.make_async_copy(rates_hbm, rates_ref, sems.at[1]),
    )

    def load(head):
        at = lanes(head)
        return (
            pltpu.make_async_copy(k_hbm.at[:, at], k_raw.at[:, at], arrived.at[0, head]),
            pltpu.make_async_copy(v_hbm.at[:, at], v_raw.at[:, at], arrived.at[1, head]),
        )

    share = sums.shape[0] // heads

    def store(head):
        pieces = pl.ds(head * share, share)
        return pltpu.make_async_copy(sums.at[pieces], sums_hbm.at[pieces], left.at[head])

    for copy in small:
        copy.start()
    for head in range(heads):
        for copy in load(head):
            copy.start()
    for copy in small:
        copy.wait()
    end_a, end_b = local_ends(starts_ref, rows, ranks)
    token = lax.broadcasted_iota(jnp.int32, (rows, E), 0)
    in_a = token <= end_a
    in_b = token <= end_b
    place = lax.broadcasted_iota(jnp.int32, (8, rows), 1)
    place_end = jnp.where(place <= end_a, end_a, jnp.where(place <= end_b, end_b, ABSENT))
    gap[...] = (jnp.minimum(place_end, rows - 1) - place).astype(f32)
    upto[0] = jnp.where(in_a, 1.0, 0.0)
    upto[1] = jnp.where(in_b, 1.0, 0.0)

    def work(head):
        at = lanes(head)
        decay = jnp.exp2(gap[...] * power_of(rates_ref, head))
        keys = silu(k_raw[:, at].T)
        values = silu_wide(v_raw[:, at])
        scaled = (keys.astype(f32) * decay[:1, :]).astype(bf16)
        spread = jnp.concatenate(
            [
                (values * upto[0]).astype(bf16),
                (values * upto[1]).astype(bf16),
                values.astype(bf16),
            ],
            axis=1,
        )
        running = jnp.dot(scaled, spread, preferred_element_type=f32)
        until_a, until_b, until_c = (running[:, x * E : (x + 1) * E] for x in range(SEGS))
        for x, part in enumerate((until_a, until_b - until_a, until_c - until_b)):
            sums[pl.ds(head * share, share), x] = part.astype(bf16).reshape(share, -1, E)

    @pl.loop(0, heads // 2)
    def _(group):
        mine = [group * 2 + index for index in range(2)]
        for head in mine:
            for copy in load(head):
                copy.wait()
        for head in mine:
            work(head)
        for head in mine:
            store(head).start()

    for head in range(heads):
        store(head).wait()


def request_ends(starts_ref, rows, ranks):
    count = starts_ref.shape[0]
    ends = [
        starts_ref[r + 1] - 1 if r + 1 < count else jnp.int32(rows * ranks - 1)
        for r in range(count)
    ]
    return ends, [end // rows for end in ends]


def advance(rows, rate, homes, got_ref, counts, keep):
    ranks = got_ref.shape[0]
    for p in range(ranks):
        counts[p] = 0
    for home in homes:
        counts[home] = counts[home] + 1
    whole = scalar_exp(float(rows) * -rate)
    state = jnp.zeros(got_ref.shape[2:], f32)
    for p in range(ranks):
        keep(p, state)
        ended = counts[p]
        state = got_ref[p, ended].astype(f32) + state * (whole * (ended == 0).astype(f32))


def my_rate(rates_ref, ranks):
    return rate_of(rates_ref, lax.axis_index("ctx") * rates_ref.shape[0] // ranks)


def scan_kernel(
    rows, starts_ref, slots_ref, rates_ref, got_ref, inner_hbm, back_ref, counts, carried
):
    ranks = got_ref.shape[0]
    rate = my_rate(rates_ref, ranks)
    ends, homes = request_ends(starts_ref, rows, ranks)

    def keep(p, state):
        carried[p] = state
        back_ref[p, 0] = state.astype(bf16)

    advance(rows, rate, homes, got_ref, counts, keep)
    for r, (end, home) in enumerate(zip(ends, homes)):
        second = home == homes[r - 1] if r else jnp.bool_(False)
        lead = scalar_exp((end - home * rows + 1).astype(f32) * -rate)
        lead = lead * jnp.where(second, 0.0, 1.0)
        final = got_ref[home, second.astype(jnp.int32)].astype(f32) + carried[home] * lead
        back_ref[slots_ref[r], 1] = final.astype(bf16)


def inner_kernel(
    rows, ranks, starts_ref, rates_ref, gain_ref, q_hbm, k_hbm, v_hbm, gate_hbm,
    inner_hbm, act_hbm, gated_hbm,
    q_raw, k_raw, v_raw, gate_raw, inner, act, gated, dist, arrived, left,
):
    heads = q_raw.shape[1] // E

    def load(head):
        at = lanes(head)
        return (
            pltpu.make_async_copy(q_hbm.at[:, at], q_raw.at[:, at], arrived.at[0, head]),
            pltpu.make_async_copy(k_hbm.at[:, at], k_raw.at[:, at], arrived.at[1, head]),
            pltpu.make_async_copy(v_hbm.at[:, at], v_raw.at[:, at], arrived.at[2, head]),
            pltpu.make_async_copy(gate_hbm.at[:, at], gate_raw.at[:, at], arrived.at[3, head]),
        )

    def store(head):
        at = lanes(head)
        return (
            pltpu.make_async_copy(inner.at[:, at], inner_hbm.at[:, at], left.at[0, head]),
            pltpu.make_async_copy(act.at[:, at], act_hbm.at[:, at], left.at[1, head]),
            pltpu.make_async_copy(gated.at[:, at], gated_hbm.at[:, at], left.at[2, head]),
        )

    for head in range(heads):
        for copy in load(head):
            copy.start()
    end_a, end_b = local_ends(starts_ref, rows, ranks)
    for block in range(rows // BLOCK):
        t = lax.broadcasted_iota(jnp.int32, (BLOCK, BLOCK), 0)
        s = lax.broadcasted_iota(jnp.int32, (BLOCK, BLOCK), 1)
        here = t + block * BLOCK
        begin = jnp.where(here <= end_a, 0, jnp.where(here <= end_b, end_a + 1, end_b + 1))
        keep = (s <= t) & (s + block * BLOCK >= begin)
        dist[block] = jnp.where(keep, (t - s).astype(f32), FAR)

    place = lax.broadcasted_iota(jnp.int32, (8, BLOCK), 1)
    begin = jnp.where(
        BLOCK - 1 <= end_a, 0, jnp.where(BLOCK - 1 <= end_b, end_a + 1, end_b + 1)
    )
    gap = jnp.where(place >= begin, (BLOCK - 1 - place).astype(f32), FAR)

    @pl.loop(0, heads)
    def _(head):
        at = lanes(head)
        power = power_of(rates_ref, head)
        for copy in load(head):
            copy.wait()
        act[:, at] = silu(q_raw[:, at])
        opened = 1.0 + jnp.tanh(0.5 * gate_raw[:, at].astype(f32))
        gated[:, at] = opened * (0.5 * gain_ref[:, at])
        keys = silu(k_raw[:, at])
        values = silu(v_raw[:, at])
        decay = jnp.exp2(gap * power)
        turned = (keys[:BLOCK].T.astype(f32) * decay[:1, :]).astype(bf16)
        inner[pl.ds(rows, E), at] = jnp.dot(turned, values[:BLOCK], preferred_element_type=f32)
        for block in range(rows // BLOCK):
            base = block * BLOCK
            for top in range(0, BLOCK, TILE):
                wide = top + TILE
                mine = pl.ds(base + top, TILE)
                scores = lax.dot_general(
                    act[mine, at],
                    keys[base : base + wide],
                    (((1,), (1,)), ((), ())),
                    preferred_element_type=f32,
                )
                decay = jnp.exp2(dist[block, top : top + TILE, :wide] * power)
                weights = (scores * decay).astype(bf16)
                inner[mine, at] = jnp.dot(
                    weights, values[base : base + wide], preferred_element_type=f32
                )
        for copy in store(head):
            copy.start()

    for head in range(heads):
        for copy in store(head):
            copy.wait()


def outer_kernel(
    rows, ranks, starts_ref, rates_ref, back_ref, act_ref, inner_ref,
    out_ref, final_hbm, squares_ref, total, lead, handed, left,
):
    heads = inner_ref.shape[1] // E
    share = back_ref.shape[0] // heads
    finals = pltpu.make_async_copy(back_ref.at[:, 1], final_hbm, left.at[0])
    finals.start()
    end_a, end_b = local_ends(starts_ref, rows, ranks)
    mid_end = jnp.where(end_a >= BLOCK - 1, end_a, jnp.where(end_b >= BLOCK - 1, end_b, ABSENT))
    from_before = (end_a >= BLOCK - 1).astype(f32)
    total[...] = jnp.zeros_like(total)
    steps = lax.broadcasted_iota(jnp.int32, (BLOCK, E), 0)
    for block, last in enumerate((end_a, mid_end)):
        here = steps + block * BLOCK <= last
        lead[block] = jnp.where(here, (steps + 1).astype(f32), FAR)

    for head in range(heads):
        incoming = back_ref[pl.ds(head * share, share), 0].reshape(E, E).astype(f32)
        whole = scalar_exp2(float(BLOCK) * power_of(rates_ref, head)) * from_before
        later = inner_ref[pl.ds(rows, E), head * E : (head + 1) * E] + incoming * whole
        handed[head] = later.astype(bf16)

    @pl.loop(0, heads, unroll=4)
    def _(head):
        at = lanes(head)
        power = power_of(rates_ref, head)
        incoming = back_ref[pl.ds(head * share, share), 0].reshape(E, E)
        for block, state in enumerate((incoming, handed[head])):
            span = pl.ds(block * BLOCK, BLOCK)
            outer = jnp.dot(act_ref[span, at], state, preferred_element_type=f32)
            attended = inner_ref[span, at] + outer * jnp.exp2(lead[block] * power)
            out_ref[span, at] = attended
            total[span, :] += attended * attended

    row_sums = jnp.concatenate(
        [
            jnp.sum(total[first : first + E, :].T, axis=0, keepdims=True)
            for first in range(0, rows, E)
        ],
        axis=0,
    )
    squares_ref[...] = jnp.broadcast_to(row_sums[None], squares_ref.shape)
    finals.wait()


def norm_kernel(
    features, squares_ref, att_ref, gated_ref, out_hbm, out, sems
):
    bands = out.shape[0] // E

    def store(band):
        span = pl.ds(band * E, E)
        return pltpu.make_async_copy(out.at[span, :], out_hbm.at[span, :], sems.at[band])

    total = jnp.sum(squares_ref[...], axis=0)
    scale = lax.rsqrt(total * (1.0 / features) + norm_eps)
    for band in range(bands):
        span = pl.ds(band * E, E)
        column = jnp.broadcast_to(scale[band : band + 1], (E, E)).T
        for first in range(0, out.shape[1], E):
            cols = slice(first, first + E)
            out[span, cols] = (att_ref[span, cols] * column * gated_ref[span, cols]).astype(bf16)
        store(band).start()
    for band in range(bands):
        store(band).wait()


def cost(flops, moved, hard):
    return pl.CostEstimate(flops=int(flops), bytes_accessed=int(moved), transcendentals=int(hard))


def swap(array, axis):
    return lax.all_to_all(array, axis, split_axis=0, concat_axis=0, tiled=True)


def per_device(
    query, key_in, value_in, gate_in, norm_gain, decay_rate, request_starts, request_slots
):
    return local(
        lax.axis_size("ctx"), lax.axis_size("head"), query, key_in, value_in, gate_in, norm_gain,
        decay_rate, request_starts, request_slots,
    )


def local(
    ranks, groups, query, key_in, value_in, gate_in, norm_gain, decay_rate, request_starts,
    request_slots,
):
    rows, width = query.shape
    heads = decay_rate.shape[0]
    piece = E * heads // ranks

    sums = pl.pallas_call(
        functools.partial(states_kernel, rows, ranks),
        out_shape=jax.ShapeDtypeStruct((ranks, SEGS, piece, E), bf16),
        in_specs=[HBM, HBM, HBM, HBM],
        out_specs=HBM,
        scratch_shapes=[
            pltpu.SMEM(request_starts.shape, jnp.int32),
            pltpu.SMEM(decay_rate.shape, f32),
            pltpu.VMEM((rows, width), bf16),
            pltpu.VMEM((rows, width), bf16),
            pltpu.VMEM((8, rows), f32),
            pltpu.VMEM((ENDS_MOST, rows, E), f32),
            pltpu.VMEM((ranks, SEGS, piece, E), bf16),
            pltpu.SemaphoreType.DMA((2,)),
            pltpu.SemaphoreType.DMA((2, heads)),
            pltpu.SemaphoreType.DMA((heads,)),
        ],
        compiler_params=pltpu.CompilerParams(vmem_limit_bytes=LIMIT),
        cost_estimate=cost(2 * rows * width * E * SEGS, 5 * MIB, 3 * rows * width),
        name="states",
    )(request_starts, decay_rate, key_in, value_in)

    got = swap(sums, "ctx")

    inner, act, gated = pl.pallas_call(
        functools.partial(inner_kernel, rows, ranks),
        out_shape=(
            jax.ShapeDtypeStruct((rows + E, width), f32),
            jax.ShapeDtypeStruct((rows, width), bf16),
            jax.ShapeDtypeStruct((rows, width), f32),
        ),
        in_specs=[SMEM, SMEM, VMEM, HBM, HBM, HBM, HBM],
        out_specs=(HBM, HBM, HBM),
        scratch_shapes=[
            pltpu.VMEM((rows, width), bf16),
            pltpu.VMEM((rows, width), bf16),
            pltpu.VMEM((rows, width), bf16),
            pltpu.VMEM((rows, width), bf16),
            pltpu.VMEM((rows + E, width), f32),
            pltpu.VMEM((rows, width), bf16),
            pltpu.VMEM((rows, width), f32),
            pltpu.VMEM((rows // BLOCK, BLOCK, BLOCK), f32),
            pltpu.SemaphoreType.DMA((4, heads)),
            pltpu.SemaphoreType.DMA((3, heads)),
        ],
        compiler_params=pltpu.CompilerParams(vmem_limit_bytes=LIMIT),
        cost_estimate=cost(4 * rows * width * BLOCK, 12 * rows * width, rows * width * 8),
        name="inner",
    )(request_starts, decay_rate, norm_gain.reshape(1, width), query, key_in, value_in, gate_in)

    back = pl.pallas_call(
        functools.partial(scan_kernel, rows),
        out_shape=jax.ShapeDtypeStruct((ranks, 2, piece, E), bf16),
        in_specs=[SMEM, SMEM, SMEM, VMEM, HBM],
        out_specs=VMEM,
        scratch_shapes=[pltpu.SMEM((ranks,), jnp.int32), pltpu.VMEM((ranks, piece, E), f32)],
        compiler_params=pltpu.CompilerParams(vmem_limit_bytes=50 * MIB),
        cost_estimate=cost(MIB, 2 * MIB, 0),
        name="scan",
    )(request_starts, request_slots, decay_rate, got, inner)

    returned = swap(back, "ctx")

    attended, final_states, squares = pl.pallas_call(
        functools.partial(outer_kernel, rows, ranks),
        out_shape=(
            jax.ShapeDtypeStruct((rows + E, width), f32),
            jax.ShapeDtypeStruct((ranks, piece, E), bf16),
            jax.ShapeDtypeStruct((groups, rows // E, E), f32),
        ),
        in_specs=[SMEM, SMEM, VMEM, VMEM, VMEM],
        out_specs=(VMEM, HBM, VMEM),
        scratch_shapes=[
            pltpu.VMEM((rows, E), f32),
            pltpu.VMEM((rows // BLOCK, BLOCK, E), f32),
            pltpu.VMEM((heads, E, E), bf16),
            pltpu.SemaphoreType.DMA((1,)),
        ],
        input_output_aliases={4: 0},
        compiler_params=pltpu.CompilerParams(vmem_limit_bytes=ROOM),
        cost_estimate=cost(2 * rows * width * E, 10 * MIB, MIB),
        name="outer",
    )(request_starts, decay_rate, returned, act, inner)

    shared = swap(squares, "head")

    normed_output = pl.pallas_call(
        functools.partial(norm_kernel, float(width * groups)),
        out_shape=jax.ShapeDtypeStruct((rows, width), bf16),
        in_specs=[VMEM, VMEM, VMEM],
        out_specs=HBM,
        scratch_shapes=[
            pltpu.VMEM((rows, width), bf16),
            pltpu.SemaphoreType.DMA((rows // E,)),
        ],
        compiler_params=pltpu.CompilerParams(vmem_limit_bytes=ROOM),
        cost_estimate=cost(6 * rows * width, 8 * MIB, rows * width),
        name="norm",
    )(shared, attended, gated)
    return (normed_output, final_states.reshape(1, heads, E, E))


def solution(mesh):
    placed = (
        P("ctx", "head"),
        P("ctx", "head"),
        P("ctx", "head"),
        P("ctx", "head"),
        P("head"),
        P("head"),
        P(),
        P(),
    )
    return jax.shard_map(
        per_device,
        mesh=mesh,
        in_specs=placed,
        out_specs=(P("ctx", "head"), P("ctx", "head", None, None)),
        check_vma=False,
    )
```
